512 devices in a mesh: blk: 32 (over z_hi, x, core), head: 16 (over y, z_lo).
Axes of the slice: x: 4, y: 4, z: 16 (z_hi: 4, z_lo: 4; z = z_hi * 4 + z_lo), core: 2. Of those that a mesh axis runs over, the one named last changes fastest.
Arguments:
- query: bfloat16 [4096, 128, 128], P(('blk', 'head')), may hold values from -24 to 24
- key: bfloat16 [4096, 8, 128], P(('blk', 'head')), may hold values from -18 to 18
- value: bfloat16 [4096, 8, 128], P(('blk', 'head')), may hold values from -6 to 6
- out_grad: bfloat16 [4096, 128, 128], P(('blk', 'head')), may hold values from -6 to 6
- block_order: int32 [64], replicated, may hold values from 0 to 63, each once
Outputs:
- query_grad: bfloat16 [4096, 128, 128], P(('blk', 'head'))
- key_grad: bfloat16 [4096, 8, 128], P(('blk', 'head'))
- value_grad: bfloat16 [4096, 8, 128], P(('blk', 'head'))
The draws below stay inside these ranges and needn't reach their ends.
Inputs may be any that keep to these rules, and one draw needn't show every extreme that they name: `block_order`: each value appears once.
All inputs are finite; a program needn't handle non-finite values.
Results may differ from the reference program's by a relative error of at most 0.012.
Values may be sent and summed in bfloat16 or wider, within the bound.
A program may use at most 64 MiB of HBM per device.

```python
import jax
import jax.numpy as jnp
from jax import lax

DH = 128
HQ = 128
HK = 8
CH = 64
S = 4096
GROUP = 16
N_BLK = 32


def draw_query(key, part):
    key = jax.random.fold_in(key, 5)
    values = jnp.clip(jax.random.normal(key, (S, HQ, DH), jnp.float32), -6.0, 6.0)
    return values.astype(jnp.bfloat16)


def draw_key(key, part):
    key = jax.random.fold_in(key, 9)
    values = 3.0 * jnp.clip(jax.random.normal(key, (S, HK, DH), jnp.float32), -6.0, 6.0)
    return values.astype(jnp.bfloat16)


def block_levels(own_key, shape, split, smallest, top_value):
    def one(position, shards_of):
        draws = jax.random.uniform(jax.random.fold_in(jax.random.fold_in(own_key, 6), position), (shards_of,), jnp.float32, smallest / len(split), top_value / len(split))
        return jnp.repeat(jnp.exp(draws), shape[position] // shards_of).reshape((-1,) + (1,) * (len(shape) - position - 1))

    level = one(*split[0])
    for cut in split[1:]:
        level = level * one(*cut)
    return level


def normal_values(key, extent, scale, reach, split=(), kind=jnp.bfloat16):
    entries = scale * jax.random.normal(key, extent, jnp.float32)
    if split:
        entries = entries * block_levels(key, extent, split, -0.22, 0.18)
    return jnp.clip(entries, -reach, reach).astype(kind)


def setup_inputs(seed: int = 0) -> dict:
    arg_keys = jax.random.split(jax.random.key(seed), 6)
    query = draw_query(jax.random.fold_in(arg_keys[5], 71), 0)
    key = draw_key(jax.random.fold_in(arg_keys[5], 71), 0)
    value = normal_values(arg_keys[2], (S, HK, DH), 1.0, 6.0, ((0, 512),))
    out_grad = normal_values(arg_keys[3], (S, HQ, DH), 1.0, 6.0, ((0, 512),))
    block_order = jax.random.permutation(arg_keys[4], 2 * N_BLK).astype(jnp.int32)
    return {"query": query, "key": key, "value": value, "out_grad": out_grad, "block_order": block_order}


def reference(query, key, value, out_grad, block_order):
    seq_len = query.shape[0]
    slots = jnp.arange(seq_len).astype(jnp.int32)
    positions = block_order[slots // CH].astype(jnp.int32) * CH + slots % CH
    allowed = positions[None, :] <= positions[:, None]
    score_scale = DH ** -0.5

    def kv_group(kv_index):
        k_mat = key[:, kv_index].astype(jnp.float32)
        v_mat = value[:, kv_index].astype(jnp.float32)

        def one_head(carry, member):
            dk_acc, dv_acc = carry
            head_index = kv_index * GROUP + member
            q_mat = query[:, head_index].astype(jnp.float32)
            g_mat = out_grad[:, head_index].astype(jnp.float32)
            logits = jnp.dot(q_mat, k_mat.T, preferred_element_type=jnp.float32) * score_scale
            log_norm = jax.nn.logsumexp(jnp.where(allowed, logits, -jnp.inf), axis=1)
            probs = jnp.where(allowed, jnp.exp(logits - log_norm[:, None]), 0.0)
            probs_low = lax.optimization_barrier(probs.astype(jnp.bfloat16)).astype(jnp.float32)
            attn_out = jnp.dot(probs_low, v_mat, preferred_element_type=jnp.float32)
            delta = jnp.sum(g_mat * attn_out, axis=1)
            dprobs = jnp.dot(g_mat, v_mat.T, preferred_element_type=jnp.float32)
            dscores = probs * (dprobs - delta[:, None])
            dscores = lax.optimization_barrier(dscores.astype(jnp.bfloat16)).astype(jnp.float32)
            dq_head = (jnp.dot(dscores, k_mat, preferred_element_type=jnp.float32) * score_scale).astype(jnp.bfloat16)
            dk_acc = dk_acc + jnp.dot(dscores.T, q_mat, preferred_element_type=jnp.float32) * score_scale
            dv_acc = dv_acc + jnp.dot(probs_low.T, g_mat, preferred_element_type=jnp.float32)
            return (dk_acc, dv_acc), dq_head

        zeros = jnp.zeros((seq_len, DH), jnp.float32)
        (dk_sum, dv_sum), dq_stack = lax.scan(one_head, (zeros, zeros), jnp.arange(GROUP).astype(jnp.int32))
        return dq_stack, dk_sum.astype(jnp.bfloat16), dv_sum.astype(jnp.bfloat16)

    dq_all, dk_all, dv_all = lax.map(kv_group, jnp.arange(HK).astype(jnp.int32))
    query_grad = jnp.transpose(dq_all, (2, 0, 1, 3)).reshape(seq_len, HQ, DH)
    key_grad = jnp.transpose(dk_all, (1, 0, 2))
    value_grad = jnp.transpose(dv_all, (1, 0, 2))
    return (query_grad, key_grad, value_grad)
```

```python
import functools

import jax
import jax.numpy as jnp
from jax import lax
from jax.experimental import pallas as pl
from jax.experimental.pallas import tpu as pltpu
from jax.sharding import PartitionSpec as P

MESH = pl.DeviceIdType.MESH
F32 = jnp.float32
BF16 = jnp.bfloat16
NX, NY, NZ = 4, 4, 16
PLANE = NX * NY
RIGHT = NZ // 2
LEFT = NZ - 1 - RIGHT
TOK = 8
GROUP = 16
DH = 128
SEQ = 4096
BLOCKS = 64
ROWS = 1024
TILES = 4
TR = ROWS // TILES
KC = 512
SCALE = DH ** -0.5


def place():
    blk = lax.axis_index("blk")
    head = lax.axis_index("head")
    z = (blk // 8) * 4 + head % 4
    return (blk // 2) % 4, head // 4, z, blk % 2


def device(x, y, z, c):
    return (((z // 4) * 4 + x) * 2 + c, y * 4 + z % 4)


def kv_head(x, y):
    return (y // 2) * 4 + (x % 2) * 2 + y % 2


def group_peer(x, m):
    return (x // 2) * 2 + (m // 2) % 2, (m // 4) * 2 + m % 2


def meet(x, y, z, c):
    barrier = pltpu.get_barrier_semaphore()
    i = x * NY + y
    for d in range(1, PLANE):
        j = (i + d) % PLANE
        pl.semaphore_signal(barrier, inc=1, device_id=device(j // NY, j % NY, z, c), device_id_type=MESH)
    for to in (device(x, y, (z + 1) % NZ, c), device(x, y, (z + NZ - 1) % NZ, c), device(x, y, z, 1 - c)):
        pl.semaphore_signal(barrier, inc=1, device_id=to, device_id_type=MESH)
    pl.semaphore_wait(barrier, PLANE - 1 + 3)


def send(src, dst, send_sem, recv_sem, to):
    copy = pltpu.make_async_remote_copy(
        src_ref=src, dst_ref=dst, send_sem=send_sem, recv_sem=recv_sem, device_id=to, device_id_type=MESH
    )
    return copy


def gather_kernel(q_ref, g_ref, kv_ref, qg_ref, gg_ref, kvg_ref, q_s, q_r, g_s, g_r, p_s, p_r, r_s, r_r, l_s, l_r, c_s, c_r, own):
    x, y, z, c = place()
    i = x * NY + y
    m = kv_head(x, y)
    right = device(x, y, (z + 1) % NZ, c)
    left = device(x, y, (z + NZ - 1) % NZ, c)
    other = device(x, y, z, 1 - c)
    meet(x, y, z, c)
    sends = []

    def start(src, dst, ss, rs, to):
        copy = send(src, dst, ss, rs, to)
        copy.start()
        sends.append(copy)

    for d in range(1, PLANE):
        j = (i + d) % PLANE
        start(kv_ref.at[kv_head(j // NY, j % NY)], kvg_ref.at[z, c, i], p_s.at[d], p_r.at[d], device(j // NY, j % NY, z, c))
    kv_own = pltpu.make_async_copy(kv_ref.at[m], kvg_ref.at[z, c, i], own.at[0])
    kv_own.start()
    q_own = pltpu.make_async_copy(q_ref.at[:, pl.ds(m * GROUP, GROUP), :], qg_ref.at[m], own.at[1])
    g_own = pltpu.make_async_copy(g_ref.at[:, pl.ds(m * GROUP, GROUP), :], gg_ref.at[m], own.at[2])
    q_own.start()
    g_own.start()
    for d in range(1, 8):
        n = (m + d) % 8
        px, py = group_peer(x, n)
        to = device(px, py, z, c)
        start(q_ref.at[:, pl.ds(n * GROUP, GROUP), :], qg_ref.at[m], q_s.at[d], q_r.at[d], to)
        start(g_ref.at[:, pl.ds(n * GROUP, GROUP), :], gg_ref.at[m], g_s.at[d], g_r.at[d], to)

    kv_own.wait()
    for d in range(1, PLANE):
        j = (i + PLANE - d) % PLANE
        send(kv_ref.at[0], kvg_ref.at[z, c, j], p_s.at[d], p_r.at[d], other).wait_recv()

    for k in range(RIGHT + 1):
        zr = (z + NZ - k) % NZ
        if k:
            send(kvg_ref.at[zr, c], kvg_ref.at[zr, c], r_s.at[k - 1], r_r.at[k - 1], right).wait_recv()
        if k < RIGHT:
            start(kvg_ref.at[zr, c], kvg_ref.at[zr, c], r_s.at[k], r_r.at[k], right)
        start(kvg_ref.at[zr, c], kvg_ref.at[zr, c], c_s.at[k], c_r.at[k], other)
        if k <= LEFT:
            zl = (z + k) % NZ
            if k:
                send(kvg_ref.at[zl, c], kvg_ref.at[zl, c], l_s.at[k - 1], l_r.at[k - 1], left).wait_recv()
            if k < LEFT:
                start(kvg_ref.at[zl, c], kvg_ref.at[zl, c], l_s.at[k], l_r.at[k], left)
            if k:
                start(kvg_ref.at[zl, c], kvg_ref.at[zl, c], c_s.at[RIGHT + k], c_r.at[RIGHT + k], other)

    q_own.wait()
    g_own.wait()
    for d in range(1, 8):
        n = (m + 8 - d) % 8
        send(qg_ref.at[n], qg_ref.at[n], q_s.at[d], q_r.at[d], other).wait_recv()
        send(gg_ref.at[n], gg_ref.at[n], g_s.at[d], g_r.at[d], other).wait_recv()
    for k in range(NZ):
        zk = (z + NZ - k) % NZ if k <= RIGHT else (z + k - RIGHT) % NZ
        send(kvg_ref.at[zk, 1 - c], kvg_ref.at[zk, 1 - c], c_s.at[k], c_r.at[k], other).wait_recv()
    for copy in sends:
        copy.wait_send()


def gather(q, g, kv):
    sem = pltpu.SemaphoreType.DMA
    return pl.pallas_call(
        gather_kernel,
        out_shape=(
            jax.ShapeDtypeStruct((8, TOK, GROUP, DH), BF16),
            jax.ShapeDtypeStruct((8, TOK, GROUP, DH), BF16),
            jax.ShapeDtypeStruct((NZ, 2, PLANE, 16, DH), BF16),
        ),
        in_specs=[pl.BlockSpec(memory_space=pltpu.VMEM)] * 3,
        out_specs=[pl.BlockSpec(memory_space=pltpu.VMEM)] * 3,
        scratch_shapes=[
            sem((8,)), sem((8,)), sem((8,)), sem((8,)), sem((PLANE,)), sem((PLANE,)),
            sem((RIGHT,)), sem((RIGHT,)), sem((LEFT,)), sem((LEFT,)), sem((NZ,)), sem((NZ,)), sem((3,)),
        ],
        compiler_params=pltpu.CompilerParams(collective_id=0, has_side_effects=True, vmem_limit_bytes=32 << 20),
        name="gather_qkv",
    )(q, g, kv)


def dot(a, b, dims):
    return lax.dot_general(a, b, (dims, ((), ())), preferred_element_type=F32)


def attend_kernel(order_ref, inv_ref, q_ref, g_ref, kvg_ref, dq_ref, dkv_ref, ks, kt, vs, s_ref, dp_ref, dk, dv):
    x, y, z, c = place()

    def sort_block(p, carry):
        sb = inv_ref[p]
        b = sb // 2
        tiles = []
        for yy in range(2):
            for lo in range(4):
                tiles.append(kvg_ref[(b // 8) * 4 + lo, b % 2, ((b // 2) % 4) * NY + (sb % 2) * 2 + yy])
        both = jnp.stack(tiles).astype(F32).reshape(8, 2, 8, DH)
        rows = pl.ds(pl.multiple_of(p * 64, 64), 64)
        ks[rows, :] = both[:, 0].reshape(64, DH).astype(BF16)
        vs[rows, :] = both[:, 1].reshape(64, DH).astype(BF16)
        return carry

    lax.fori_loop(0, BLOCKS, sort_block, 0)
    for n in range(SEQ // KC):
        kt[:, n * KC:(n + 1) * KC] = ks[n * KC:(n + 1) * KC, :].T
    dk[...] = jnp.zeros_like(dk)
    dv[...] = jnp.zeros_like(dv)

    for t in range(TILES):
        sb = ((z // 4 * 4 + (x // 2) * 2 + t % 2) * 2 + c) * 2 + t // 2
        pos = order_ref[sb]
        count = pos // (KC // 64) + 1
        q = q_ref[t * TR:(t + 1) * TR, :]
        g = g_ref[t * TR:(t + 1) * TR, :]
        qt = q.T
        gt = g.T
        lane = lax.broadcasted_iota(jnp.int32, (1, TR), 1)
        limit = pos * 64 + (lane // 128) * 32 + (z % 4) * 8 + (lane // 16) % 8

        def scores(n, top):
            rows = pl.ds(pl.multiple_of(n * KC, KC), KC)
            s = dot(ks[rows, :], qt, ((1,), (0,)))
            key_pos = n * KC + lax.broadcasted_iota(jnp.int32, (KC, TR), 0)
            s = jnp.where(key_pos <= limit, s, -1e30)
            s_ref[rows, :] = s
            dp_ref[rows, :] = dot(vs[rows, :], gt, ((1,), (0,)))
            return jnp.maximum(top, jnp.max(s.reshape(KC // 8, 8, TR), axis=0))

        top = lax.fori_loop(0, count, scores, jnp.full((8, TR), -1e30, F32))
        top = jnp.max(top, axis=0, keepdims=True)

        def weigh(n, carry):
            total, mixed = carry
            rows = pl.ds(pl.multiple_of(n * KC, KC), KC)
            e = jnp.exp((s_ref[rows, :] - top) * SCALE)
            s_ref[rows, :] = e
            total = total + jnp.sum(e.reshape(KC // 8, 8, TR), axis=0)
            mixed = mixed + jnp.sum((e * dp_ref[rows, :]).reshape(KC // 8, 8, TR), axis=0)
            return total, mixed

        zero = jnp.zeros((8, TR), F32)
        total, mixed = lax.fori_loop(0, count, weigh, (zero, zero))
        inverse = 1.0 / jnp.sum(total, axis=0, keepdims=True)
        delta = jnp.sum(mixed, axis=0, keepdims=True) * inverse

        def grads(n, dqt):
            rows = pl.ds(pl.multiple_of(n * KC, KC), KC)
            p = s_ref[rows, :] * inverse
            ds = (p * (dp_ref[rows, :] - delta)).astype(BF16)
            dv[rows, :] += dot(p.astype(BF16), g, ((1,), (0,)))
            dk[rows, :] += dot(ds, q, ((1,), (0,)))
            return dqt + dot(kt[:, rows], ds, ((1,), (0,)))

        dqt = lax.fori_loop(0, count, grads, jnp.zeros((DH, TR), F32))
        dq_ref[t * TR:(t + 1) * TR, :] = (dqt * SCALE).T.astype(BF16)

    def spread_block(sb, carry):
        p = order_ref[sb]
        b = sb // 2
        rows = pl.ds(pl.multiple_of(p * 64, 64), 64)
        both = jnp.stack([(dk[rows, :] * SCALE).reshape(8, 8, DH), dv[rows, :].reshape(8, 8, DH)], axis=1)
        tiles = both.reshape(8, 16, DH).astype(BF16)
        for yy in range(2):
            for lo in range(4):
                dkv_ref[(b // 8) * 4 + lo, b % 2, ((b // 2) % 4) * NY + (sb % 2) * 2 + yy] = tiles[yy * 4 + lo]
        return carry

    lax.fori_loop(0, BLOCKS, spread_block, 0)


def attend(order, inverse, q, g, kvg):
    vmem = pl.BlockSpec(memory_space=pltpu.VMEM)
    smem = pl.BlockSpec(memory_space=pltpu.SMEM)
    return pl.pallas_call(
        attend_kernel,
        out_shape=(
            jax.ShapeDtypeStruct((ROWS, DH), BF16),
            jax.ShapeDtypeStruct((NZ, 2, PLANE, 16, DH), BF16),
        ),
        in_specs=[smem, smem, vmem, vmem, vmem],
        out_specs=[vmem, vmem],
        scratch_shapes=[
            pltpu.VMEM((SEQ, DH), BF16),
            pltpu.VMEM((DH, SEQ), BF16),
            pltpu.VMEM((SEQ, DH), BF16),
            pltpu.VMEM((SEQ, TR), F32),
            pltpu.VMEM((SEQ, TR), F32),
            pltpu.VMEM((SEQ, DH), F32),
            pltpu.VMEM((SEQ, DH), F32),
        ],
        compiler_params=pltpu.CompilerParams(vmem_limit_bytes=48 << 20),
        name="attend",
    )(order, inverse, q, g, kvg)


def reduce_kernel(dq_ref, dkv_ref, dqh_ref, dkvh_ref, cx, rr, rst, lr, lst, fin, fst, q_s, q_r, p_s, p_r, r_s, r_r, l_s, l_r, c_s, c_r, own):
    x, y, z, c = place()
    i = x * NY + y
    m = kv_head(x, y)
    right = device(x, y, (z + 1) % NZ, c)
    left = device(x, y, (z + NZ - 1) % NZ, c)
    other = device(x, y, z, 1 - c)
    meet(x, y, z, c)
    sends = []

    def start(src, dst, ss, rs, to):
        copy = send(src, dst, ss, rs, to)
        copy.start()
        sends.append(copy)

    order = []
    for k in range(RIGHT):
        order.append((z + RIGHT - k) % NZ)
        if k < LEFT:
            order.append((z + NZ - LEFT + k) % NZ)
    order.append(z)
    for n, dest in enumerate(order):
        start(dkv_ref.at[dest, 1 - c], cx.at[dest], c_s.at[n], c_r.at[n], other)
    q_own = pltpu.make_async_copy(dq_ref.at[m], dqh_ref.at[:, pl.ds(m * GROUP, GROUP), :], own.at[0])
    q_own.start()
    for d in range(1, 8):
        n = (m + d) % 8
        px, py = group_peer(x, n)
        start(dq_ref.at[n], dqh_ref.at[:, pl.ds(m * GROUP, GROUP), :], q_s.at[d], q_r.at[d], device(px, py, z, c))

    def mine(n):
        dest = order[n]
        send(cx.at[dest], cx.at[dest], c_s.at[n], c_r.at[n], other).wait_recv()
        return dkv_ref[dest, c].astype(F32) + cx[dest].astype(F32)

    n = 0
    for k in range(RIGHT):
        total = mine(n)
        n += 1
        if k:
            send(rr.at[k - 1], rr.at[k - 1], r_s.at[k - 1], r_r.at[k - 1], right).wait_recv()
            total = total + rr[k - 1].astype(F32)
        rst[k] = total.astype(BF16)
        start(rst.at[k], rr.at[k], r_s.at[k], r_r.at[k], right)
        if k < LEFT:
            total = mine(n)
            n += 1
            if k:
                send(lr.at[k - 1], lr.at[k - 1], l_s.at[k - 1], l_r.at[k - 1], left).wait_recv()
                total = total + lr[k - 1].astype(F32)
            lst[k] = total.astype(BF16)
            start(lst.at[k], lr.at[k], l_s.at[k], l_r.at[k], left)
    total = mine(n)
    send(lr.at[LEFT - 1], lr.at[LEFT - 1], l_s.at[LEFT - 1], l_r.at[LEFT - 1], left).wait_recv()
    total = total + lr[LEFT - 1].astype(F32)
    send(rr.at[RIGHT - 1], rr.at[RIGHT - 1], r_s.at[RIGHT - 1], r_r.at[RIGHT - 1], right).wait_recv()
    total = total + rr[RIGHT - 1].astype(F32)
    fst[...] = total.astype(BF16)
    for d in range(1, PLANE):
        j = (i + d) % PLANE
        start(fst.at[j], fin.at[i], p_s.at[d], p_r.at[d], device(j // NY, j % NY, z, c))
    p_own = pltpu.make_async_copy(fst.at[i], fin.at[i], own.at[1])
    p_own.start()
    p_own.wait()
    for d in range(1, PLANE):
        j = (i + PLANE - d) % PLANE
        send(fin.at[j], fin.at[j], p_s.at[d], p_r.at[d], other).wait_recv()
    for n in range(8):
        px, py = (n // 2) % 2, (n // 4) * 2 + n % 2
        total = fin[px * NY + py].astype(F32) + fin[(px + 2) * NY + py].astype(F32)
        dkvh_ref[n] = total.astype(BF16)
    q_own.wait()
    for d in range(1, 8):
        n = (m + 8 - d) % 8
        send(dq_ref.at[n], dqh_ref.at[:, pl.ds(n * GROUP, GROUP), :], q_s.at[d], q_r.at[d], other).wait_recv()
    for copy in sends:
        copy.wait_send()


def reduce(dq, dkv):
    sem = pltpu.SemaphoreType.DMA
    block = (PLANE, 16, DH)
    return pl.pallas_call(
        reduce_kernel,
        out_shape=(
            jax.ShapeDtypeStruct((TOK, 8 * GROUP, DH), BF16),
            jax.ShapeDtypeStruct((8, 16, DH), BF16),
        ),
        in_specs=[pl.BlockSpec(memory_space=pltpu.VMEM)] * 2,
        out_specs=[pl.BlockSpec(memory_space=pltpu.VMEM)] * 2,
        scratch_shapes=[
            pltpu.VMEM((NZ,) + block, BF16),
            pltpu.VMEM((RIGHT,) + block, BF16),
            pltpu.VMEM((RIGHT,) + block, BF16),
            pltpu.VMEM((LEFT,) + block, BF16),
            pltpu.VMEM((LEFT,) + block, BF16),
            pltpu.VMEM(block, BF16),
            pltpu.VMEM(block, BF16),
            sem((8,)), sem((8,)), sem((PLANE,)), sem((PLANE,)),
            sem((RIGHT,)), sem((RIGHT,)), sem((LEFT,)), sem((LEFT,)), sem((NZ,)), sem((NZ,)), sem((2,)),
        ],
        compiler_params=pltpu.CompilerParams(collective_id=1, has_side_effects=True, vmem_limit_bytes=32 << 20),
        name="reduce_grads",
    )(dq, dkv)


def on_device(query, key, value, out_grad, block_order):
    kv = jnp.concatenate((jnp.transpose(key, (1, 0, 2)), jnp.transpose(value, (1, 0, 2))), axis=1)
    q, g, kvg = gather(query, out_grad, kv)
    slots = jnp.arange(BLOCKS, dtype=jnp.int32)
    inverse = jnp.sum(jnp.where(block_order[None, :] == slots[:, None], slots[None, :], 0), axis=1)
    dq, dkv = attend(block_order, inverse, q.reshape(ROWS, DH), g.reshape(ROWS, DH), kvg)
    dq_home, dkv_home = reduce(dq.reshape(8, TOK, GROUP, DH), dkv)
    grads = jnp.transpose(dkv_home, (1, 0, 2))
    return dq_home, grads[:TOK], grads[TOK:]


def solution(mesh):
    rows = P(("blk", "head"), None, None)
    return jax.shard_map(
        on_device, mesh=mesh, in_specs=(rows,) * 4 + (P(),), out_specs=(rows,) * 3, check_vma=False
    )
```

```python
import jax
import jax.numpy as jnp
from jax import lax
from jax.experimental import pallas as pl
from jax.experimental.pallas import tpu as pltpu
from jax.sharding import PartitionSpec as P

MESH = pl.DeviceIdType.MESH
F32 = jnp.float32
BF16 = jnp.bfloat16
NX, NY, NZ = 4, 4, 16
NQ = NZ // 2
PEERS = 8
TOK = 8
GROUP = 16
DH = 128
SEQ = 4096
BLOCKS = 64
ROWS = 1024
TILES = 4
TR = ROWS // TILES
KC = 512
SCALE = DH ** -0.5


def place():
    blk = lax.axis_index("blk")
    head = lax.axis_index("head")
    z = (blk // 8) * 4 + head % 4
    return (blk // 2) % 4, head // 4, z, blk % 2


def device(x, y, z, c):
    return (((z // 4) * 4 + x) * 2 + c, y * 4 + z % 4)


def peer(x, z, c, n):
    return device(x, n // 2, (z // 2) * 2 + n % 2, c)


def meet(x, y, z, c):
    barrier = pltpu.get_barrier_semaphore()
    m = y * 2 + z % 2
    to = [peer(x, z, c, (m + d) % PEERS) for d in range(1, PEERS)]
    to += [device(x, y, (z + 2 * d) % NZ, c) for d in range(1, NQ)]
    to += [device((x + d) % NX, y, z, c) for d in range(1, NX)]
    to += [device(x, y, z, 1 - c)]
    for one in to:
        pl.semaphore_signal(barrier, inc=1, device_id=one, device_id_type=MESH)
    pl.semaphore_wait(barrier, len(to))


def send(src, dst, send_sem, recv_sem, to):
    copy = pltpu.make_async_remote_copy(
        src_ref=src, dst_ref=dst, send_sem=send_sem, recv_sem=recv_sem, device_id=to, device_id_type=MESH
    )
    return copy


Z_ORDER = (1, 7, 2, 6, 3, 5, 4)
X_ORDER = (1, 3, 2)


def gather_kernel(q_ref, g_ref, kv_ref, qg_ref, gg_ref, kvg_ref, q_s, q_r, g_s, g_r, p_s, p_r, z_s, z_r, x_s, x_r, c_s, c_r, own):
    x, y, z, c = place()
    m = y * 2 + z % 2
    zq = z // 2
    other = device(x, y, z, 1 - c)
    meet(x, y, z, c)
    sends = []

    def start(src, dst, ss, rs, to):
        copy = send(src, dst, ss, rs, to)
        copy.start()
        sends.append(copy)

    def arrived(dst, ss, rs):
        send(dst, dst, ss, rs, other).wait_recv()

    for d in range(1, PEERS):
        n = (m + d) % PEERS
        start(kv_ref.at[n], kvg_ref.at[zq, x, c, m], p_s.at[d], p_r.at[d], peer(x, z, c, n))
    kv_own = pltpu.make_async_copy(kv_ref.at[m], kvg_ref.at[zq, x, c, m], own.at[0])
    kv_own.start()
    q_own = pltpu.make_async_copy(q_ref.at[:, pl.ds(m * GROUP, GROUP), :], qg_ref.at[m], own.at[1])
    g_own = pltpu.make_async_copy(g_ref.at[:, pl.ds(m * GROUP, GROUP), :], gg_ref.at[m], own.at[2])
    q_own.start()
    g_own.start()
    kv_own.wait()
    for d in range(1, PEERS):
        n = (m + PEERS - d) % PEERS
        arrived(kvg_ref.at[zq, x, c, n], p_s.at[d], p_r.at[d])
    block = kvg_ref.at[zq, x, c]
    for d in Z_ORDER:
        start(block, block, z_s.at[d], z_r.at[d], device(x, y, (z + 2 * d) % NZ, c))

    def share(d):
        block = kvg_ref.at[(zq + NQ - d) % NQ, x, c]
        for e in X_ORDER:
            start(block, block, x_s.at[d, e], x_r.at[d, e], device((x + e) % NX, y, z, c))

    def swap(d):
        zk = (zq + NQ - d) % NQ
        for e in X_ORDER:
            arrived(kvg_ref.at[zk, (x + NX - e) % NX, c], x_s.at[d, e], x_r.at[d, e])
        start(kvg_ref.at[zk, :, c], kvg_ref.at[zk, :, c], c_s.at[d], c_r.at[d], other)

    share(0)
    for d in range(1, PEERS):
        n = (m + d) % PEERS
        to = peer(x, z, c, n)
        start(q_ref.at[:, pl.ds(n * GROUP, GROUP), :], qg_ref.at[m], q_s.at[d], q_r.at[d], to)
        start(g_ref.at[:, pl.ds(n * GROUP, GROUP), :], gg_ref.at[m], g_s.at[d], g_r.at[d], to)
    for d in Z_ORDER:
        arrived(kvg_ref.at[(zq + NQ - d) % NQ, x, c], z_s.at[d], z_r.at[d])
        share(d)
    for d in (0,) + Z_ORDER:
        swap(d)
    q_own.wait()
    g_own.wait()
    for d in range(1, PEERS):
        n = (m + PEERS - d) % PEERS
        arrived(qg_ref.at[n], q_s.at[d], q_r.at[d])
        arrived(gg_ref.at[n], g_s.at[d], g_r.at[d])
    for d in range(NQ):
        arrived(kvg_ref.at[(zq + NQ - d) % NQ, :, 1 - c], c_s.at[d], c_r.at[d])
    for copy in sends:
        copy.wait_send()


def gather(q, g, kv):
    sem = pltpu.SemaphoreType.DMA
    return pl.pallas_call(
        gather_kernel,
        out_shape=(
            jax.ShapeDtypeStruct((PEERS, TOK, GROUP, DH), BF16),
            jax.ShapeDtypeStruct((PEERS, TOK, GROUP, DH), BF16),
            jax.ShapeDtypeStruct((NQ, NX, 2, PEERS, 16, DH), BF16),
        ),
        in_specs=[pl.BlockSpec(memory_space=pltpu.VMEM)] * 3,
        out_specs=[pl.BlockSpec(memory_space=pltpu.VMEM)] * 3,
        scratch_shapes=[sem((8,))] * 8 + [sem((NQ, NX))] * 2 + [sem((NQ,))] * 2 + [sem((3,))],
        compiler_params=pltpu.CompilerParams(collective_id=0, has_side_effects=True, vmem_limit_bytes=32 << 20),
        name="gather_qkv",
    )(q, g, kv)


def dot(a, b, dims):
    return lax.dot_general(a, b, (dims, ((), ())), preferred_element_type=F32)


def attend_kernel(order_ref, inv_ref, q_ref, g_ref, kvg_ref, dq_ref, dkv_ref, ks, kt, vs, s_ref, dp_ref, dk, dv):
    x, y, z, c = place()

    def sort_block(p, carry):
        sb = inv_ref[p]
        b = sb // 2
        tiles = []
        for yy in range(2):
            for lo in range(4):
                tiles.append(kvg_ref[(b // 8) * 2 + lo // 2, (b // 2) % 4, b % 2, ((sb % 2) * 2 + yy) * 2 + lo % 2])
        both = jnp.stack(tiles).astype(F32).reshape(8, 2, 8, DH)
        rows = pl.ds(pl.multiple_of(p * 64, 64), 64)
        ks[rows, :] = both[:, 0].reshape(64, DH).astype(BF16)
        vs[rows, :] = both[:, 1].reshape(64, DH).astype(BF16)
        return carry

    lax.fori_loop(0, BLOCKS, sort_block, 0)
    for n in range(SEQ // KC):
        kt[:, n * KC:(n + 1) * KC] = ks[n * KC:(n + 1) * KC, :].T
    dk[...] = jnp.zeros_like(dk)
    dv[...] = jnp.zeros_like(dv)

    for t in range(TILES):
        sb = ((z // 4 * 4 + x) * 2 + c) * 2 + t // 2
        pos = order_ref[sb]
        count = pos // (KC // 64) + 1
        q = q_ref[t * TR:(t + 1) * TR, :]
        g = g_ref[t * TR:(t + 1) * TR, :]
        qt = q.T
        gt = g.T
        lane = lax.broadcasted_iota(jnp.int32, (1, TR), 1)
        limit = pos * 64 + (t % 2) * 32 + (z % 4 // 2) * 16 + (lane // 128) * 8 + (lane // 16) % 8

        def scores(n, top):
            rows = pl.ds(pl.multiple_of(n * KC, KC), KC)
            s = dot(ks[rows, :], qt, ((1,), (0,)))
            key_pos = n * KC + lax.broadcasted_iota(jnp.int32, (KC, TR), 0)
            s = jnp.where(key_pos <= limit, s, -1e30)
            s_ref[rows, :] = s
            dp_ref[rows, :] = dot(vs[rows, :], gt, ((1,), (0,)))
            return jnp.maximum(top, jnp.max(s.reshape(KC // 8, 8, TR), axis=0))

        top = lax.fori_loop(0, count, scores, jnp.full((8, TR), -1e30, F32))
        top = jnp.max(top, axis=0, keepdims=True)

        def weigh(n, carry):
            total, mixed = carry
            rows = pl.ds(pl.multiple_of(n * KC, KC), KC)
            e = jnp.exp((s_ref[rows, :] - top) * SCALE)
            s_ref[rows, :] = e
            total = total + jnp.sum(e.reshape(KC // 8, 8, TR), axis=0)
            mixed = mixed + jnp.sum((e * dp_ref[rows, :]).reshape(KC // 8, 8, TR), axis=0)
            return total, mixed

        zero = jnp.zeros((8, TR), F32)
        total, mixed = lax.fori_loop(0, count, weigh, (zero, zero))
        inverse = 1.0 / jnp.sum(total, axis=0, keepdims=True)
        delta = jnp.sum(mixed, axis=0, keepdims=True) * inverse

        def grads(n, dqt):
            rows = pl.ds(pl.multiple_of(n * KC, KC), KC)
            p = s_ref[rows, :] * inverse
            ds = (p * (dp_ref[rows, :] - delta)).astype(BF16)
            dv[rows, :] += dot(p.astype(BF16), g, ((1,), (0,)))
            dk[rows, :] += dot(ds, q, ((1,), (0,)))
            return dqt + dot(kt[:, rows], ds, ((1,), (0,)))

        dqt = lax.fori_loop(0, count, grads, jnp.zeros((DH, TR), F32))
        dq_ref[t * TR:(t + 1) * TR, :] = (dqt * SCALE).T.astype(BF16)

    def spread_block(sb, carry):
        p = order_ref[sb]
        b = sb // 2
        rows = pl.ds(pl.multiple_of(p * 64, 64), 64)
        both = jnp.stack([(dk[rows, :] * SCALE).reshape(8, 8, DH), dv[rows, :].reshape(8, 8, DH)], axis=1)
        tiles = both.reshape(8, 16, DH).astype(BF16)
        for yy in range(2):
            for lo in range(4):
                dkv_ref[(b // 8) * 2 + lo // 2, (b // 2) % 4, b % 2, ((sb % 2) * 2 + yy) * 2 + lo % 2] = tiles[yy * 4 + lo]
        return carry

    lax.fori_loop(0, BLOCKS, spread_block, 0)


def attend(order, inverse, q, g, kvg):
    vmem = pl.BlockSpec(memory_space=pltpu.VMEM)
    smem = pl.BlockSpec(memory_space=pltpu.SMEM)
    return pl.pallas_call(
        attend_kernel,
        out_shape=(
            jax.ShapeDtypeStruct((ROWS, DH), BF16),
            jax.ShapeDtypeStruct((NQ, NX, 2, PEERS, 16, DH), BF16),
        ),
        in_specs=[smem, smem, vmem, vmem, vmem],
        out_specs=[vmem, vmem],
        scratch_shapes=[
            pltpu.VMEM((SEQ, DH), BF16),
            pltpu.VMEM((DH, SEQ), BF16),
            pltpu.VMEM((SEQ, DH), BF16),
            pltpu.VMEM((SEQ, TR), F32),
            pltpu.VMEM((SEQ, TR), F32),
            pltpu.VMEM((SEQ, DH), F32),
            pltpu.VMEM((SEQ, DH), F32),
        ],
        compiler_params=pltpu.CompilerParams(vmem_limit_bytes=48 << 20),
        name="attend",
    )(order, inverse, q, g, kvg)


def reduce_kernel(dq_ref, dkv_ref, dqh_ref, dkvh_ref, cx, xst, xr, zst, zr, fst, q_s, q_r, p_s, p_r, z_s, z_r, x_s, x_r, c_s, c_r, own):
    x, y, z, c = place()
    m = y * 2 + z % 2
    zq = z // 2
    other = device(x, y, z, 1 - c)
    meet(x, y, z, c)
    sends = []

    def start(src, dst, ss, rs, to):
        copy = send(src, dst, ss, rs, to)
        copy.start()
        sends.append(copy)

    def arrived(dst, ss, rs):
        send(dst, dst, ss, rs, other).wait_recv()

    order = Z_ORDER[::-1] + (0,)
    for d in order:
        zk = (zq + d) % NQ
        start(dkv_ref.at[zk, :, 1 - c], cx.at[d], c_s.at[d], c_r.at[d], other)
    q_own = pltpu.make_async_copy(dq_ref.at[m], dqh_ref.at[:, pl.ds(m * GROUP, GROUP), :], own.at[0])
    q_own.start()
    for d in order:
        zk = (zq + d) % NQ
        arrived(cx.at[d], c_s.at[d], c_r.at[d])
        for e in X_ORDER:
            xd = (x + e) % NX
            xst[d, e] = (dkv_ref[zk, xd, c].astype(F32) + cx[d, xd].astype(F32)).astype(BF16)
            start(xst.at[d, e], xr.at[d, e], x_s.at[d, e], x_r.at[d, e], device(xd, y, z, c))
    for d in range(1, PEERS):
        n = (m + d) % PEERS
        start(dq_ref.at[n], dqh_ref.at[:, pl.ds(m * GROUP, GROUP), :], q_s.at[d], q_r.at[d], peer(x, z, c, n))
    for d in order:
        zk = (zq + d) % NQ
        total = dkv_ref[zk, x, c].astype(F32) + cx[d, x].astype(F32)
        for e in X_ORDER:
            arrived(xr.at[d, e], x_s.at[d, e], x_r.at[d, e])
            total = total + xr[d, e].astype(F32)
        if d:
            zst[d] = total.astype(BF16)
            start(zst.at[d], zr.at[d], z_s.at[d], z_r.at[d], device(x, y, (z + 2 * d) % NZ, c))
    for d in Z_ORDER:
        arrived(zr.at[d], z_s.at[d], z_r.at[d])
        total = total + zr[d].astype(F32)
    fst[...] = total.astype(BF16)
    for d in range(1, PEERS):
        n = (m + d) % PEERS
        start(fst.at[n], dkvh_ref.at[m], p_s.at[d], p_r.at[d], peer(x, z, c, n))
    p_own = pltpu.make_async_copy(fst.at[m], dkvh_ref.at[m], own.at[1])
    p_own.start()
    q_own.wait()
    p_own.wait()
    for d in range(1, PEERS):
        n = (m + PEERS - d) % PEERS
        arrived(dqh_ref.at[:, pl.ds(n * GROUP, GROUP), :], q_s.at[d], q_r.at[d])
        arrived(dkvh_ref.at[n], p_s.at[d], p_r.at[d])
    for copy in sends:
        copy.wait_send()


def reduce(dq, dkv):
    sem = pltpu.SemaphoreType.DMA
    block = (PEERS, 16, DH)
    return pl.pallas_call(
        reduce_kernel,
        out_shape=(
            jax.ShapeDtypeStruct((TOK, 8 * GROUP, DH), BF16),
            jax.ShapeDtypeStruct((8, 16, DH), BF16),
        ),
        in_specs=[pl.BlockSpec(memory_space=pltpu.VMEM)] * 2,
        out_specs=[pl.BlockSpec(memory_space=pltpu.VMEM)] * 2,
        scratch_shapes=[
            pltpu.VMEM((NQ, NX) + block, BF16),
            pltpu.VMEM((NQ, NX) + block, BF16),
            pltpu.VMEM((NQ, NX) + block, BF16),
            pltpu.VMEM((NQ,) + block, BF16),
            pltpu.VMEM((NQ,) + block, BF16),
            pltpu.VMEM(block, BF16),
        ] + [sem((8,))] * 6 + [sem((NQ, NX))] * 2 + [sem((NQ,))] * 2 + [sem((2,))],
        compiler_params=pltpu.CompilerParams(collective_id=1, has_side_effects=True, vmem_limit_bytes=32 << 20),
        name="reduce_grads",
    )(dq, dkv)


def on_device(query, key, value, out_grad, block_order):
    kv = jnp.concatenate((jnp.transpose(key, (1, 0, 2)), jnp.transpose(value, (1, 0, 2))), axis=1)
    q, g, kvg = gather(query, out_grad, kv)
    slots = jnp.arange(BLOCKS, dtype=jnp.int32)
    inverse = jnp.sum(jnp.where(block_order[None, :] == slots[:, None], slots[None, :], 0), axis=1)
    dq, dkv = attend(block_order, inverse, q.reshape(ROWS, DH), g.reshape(ROWS, DH), kvg)
    dq_home, dkv_home = reduce(dq.reshape(8, TOK, GROUP, DH), dkv)
    grads = jnp.transpose(dkv_home, (1, 0, 2))
    return dq_home, grads[:TOK], grads[TOK:]


def solution(mesh):
    rows = P(("blk", "head"), None, None)
    return jax.shard_map(
        on_device, mesh=mesh, in_specs=(rows,) * 4 + (P(),), out_specs=(rows,) * 3, check_vma=False
    )
```

```python
import math

import jax
import jax.numpy as jnp
from jax import lax
from jax.experimental import pallas as pl
from jax.experimental.pallas import tpu as pltpu
from jax.sharding import PartitionSpec as P

MESH = pl.DeviceIdType.MESH
F32 = jnp.float32
BF16 = jnp.bfloat16
NX, NZ = 4, 16
NQ = NZ // 2
PEERS = 8
TOK = 8
GROUP = 16
DH = 128
TILES = 4
TR = PEERS * TOK * GROUP // TILES
CHUNKS = NX * 2 * PEERS
KEYS = CHUNKS * TOK
SCALE = DH ** -0.5
RATE = SCALE * math.log2(math.e)
Z_ORDER = (1, 7, 2, 6, 3, 5, 4)
X_ORDER = (1, 3, 2)
BACK = Z_ORDER[::-1] + (0,)


def place():
    blk = lax.axis_index("blk")
    head = lax.axis_index("head")
    z = (blk // 8) * 4 + head % 4
    return (blk // 2) % 4, head // 4, z, blk % 2


def device(x, y, z, c):
    return (((z // 4) * 4 + x) * 2 + c, y * 4 + z % 4)


def peer(x, z, c, n):
    return device(x, n // 2, (z // 2) * 2 + n % 2, c)


def dot(a, b):
    return lax.dot_general(a, b, (((1,), (0,)), ((), ())), preferred_element_type=F32)


def kernel(
    order_ref, q_ref, g_ref, kv_ref, dqh_ref, dkvh_ref,
    qa, ga, qt, gt, kvg, ks, vs, kt, pos, prob, dprob, tops, top, total, mixed, dk, dv, dqt, dqs,
    dkv, cx, xst, xr, zst, zr, fst,
    p_s, p_r, z_s, z_r, x_s, x_r, c_s, c_r, q_s, q_r, g_s, g_r,
    d_s, d_r, e_s, e_r, f_s, f_r, h_s, h_r, o_s, o_r, own,
):
    x, y, z, c = place()
    m = y * 2 + z % 2
    zq = z // 2
    other = device(x, y, z, 1 - c)
    sends = []

    def copy(src, dst, ss, rs, to):
        return pltpu.make_async_remote_copy(
            src_ref=src, dst_ref=dst, send_sem=ss, recv_sem=rs, device_id=to, device_id_type=MESH
        )

    def start(src, dst, ss, rs, to):
        one = copy(src, dst, ss, rs, to)
        one.start()
        sends.append(one)

    def arrived(dst, ss, rs):
        copy(dst, dst, ss, rs, other).wait_recv()

    barrier = pltpu.get_barrier_semaphore()
    to = [peer(x, z, c, (m + d) % PEERS) for d in range(1, PEERS)]
    to += [device(x, y, (z + 2 * d) % NZ, c) for d in range(1, NQ)]
    to += [device((x + d) % NX, y, z, c) for d in range(1, NX)]
    to += [other]
    for one in to:
        pl.semaphore_signal(barrier, inc=1, device_id=one, device_id_type=MESH)

    kv_own = pltpu.make_async_copy(kv_ref.at[m], kvg.at[zq, x, c, m], own.at[0])
    kv_own.start()
    q_own = pltpu.make_async_copy(q_ref.at[:, pl.ds(m * GROUP, GROUP), :], qa.at[m], own.at[1])
    g_own = pltpu.make_async_copy(g_ref.at[:, pl.ds(m * GROUP, GROUP), :], ga.at[m], own.at[2])
    q_own.start()
    g_own.start()

    step = lax.broadcasted_iota(jnp.int32, (TOK, DH), 0)

    def place_keys(d, carry):
        zk = (zq + NQ - d) % NQ
        for j in range(NX * 2):
            for h in range(2):
                first = order_ref[(zk // 2) * 16 + j * 2 + h] * 64 + (zk % 2) * 16
                for k in range(4):
                    at = (j * PEERS + h * 4 + k) * TOK
                    pos[d, at:at + TOK, :] = first + (k // 2) * 32 + (k % 2) * 8 + step
        return carry

    lax.fori_loop(0, NQ, place_keys, 0)
    top[...] = jnp.full_like(top, -1e30)
    total[...] = jnp.zeros_like(total)
    mixed[...] = jnp.zeros_like(mixed)
    dqt[...] = jnp.zeros_like(dqt)
    pl.semaphore_wait(barrier, len(to))

    for d in range(1, PEERS):
        n = (m + d) % PEERS
        start(kv_ref.at[n], kvg.at[zq, x, c, m], p_s.at[d], p_r.at[d], peer(x, z, c, n))
    kv_own.wait()
    for d in range(1, PEERS):
        arrived(kvg.at[zq, x, c, (m + PEERS - d) % PEERS], p_s.at[d], p_r.at[d])
    block = kvg.at[zq, x, c]
    for d in Z_ORDER:
        start(block, block, z_s.at[d], z_r.at[d], device(x, y, (z + 2 * d) % NZ, c))

    def share(d):
        block = kvg.at[(zq + NQ - d) % NQ, x, c]
        for e in X_ORDER:
            start(block, block, x_s.at[d, e], x_r.at[d, e], device((x + e) % NX, y, z, c))

    def swap(d):
        zk = (zq + NQ - d) % NQ
        for e in X_ORDER:
            arrived(kvg.at[zk, (x + NX - e) % NX, c], x_s.at[d, e], x_r.at[d, e])
        start(kvg.at[zk, :, c], kvg.at[zk, :, c], c_s.at[d], c_r.at[d], other)

    share(0)
    for d in range(1, PEERS):
        n = (m + d) % PEERS
        to = peer(x, z, c, n)
        start(q_ref.at[:, pl.ds(n * GROUP, GROUP), :], qa.at[m], q_s.at[d], q_r.at[d], to)
        start(g_ref.at[:, pl.ds(n * GROUP, GROUP), :], ga.at[m], g_s.at[d], g_r.at[d], to)

    lane = lax.broadcasted_iota(jnp.int32, (1, TR), 1)
    blk = (z // 4 * 4 + x) * 2 + c

    def take_queries():
        q_own.wait()
        g_own.wait()
        for d in range(1, PEERS):
            n = (m + PEERS - d) % PEERS
            arrived(qa.at[n], q_s.at[d], q_r.at[d])
            arrived(ga.at[n], g_s.at[d], g_r.at[d])
        for t in range(TILES):
            qt[t] = qa[2 * t:2 * t + 2].reshape(TR, DH).T
            gt[t] = ga[2 * t:2 * t + 2].reshape(TR, DH).T

    def score(d):
        zk = (zq + NQ - d) % NQ
        arrived(kvg.at[zk, :, 1 - c], c_s.at[d], c_r.at[d])
        both = kvg[zk].reshape(CHUNKS, 16, DH).astype(F32).reshape(CHUNKS, 2, TOK, DH)
        k = both[:, 0].reshape(KEYS, DH).astype(BF16)
        ks[...] = k
        kt[d] = k.T
        vs[...] = both[:, 1].reshape(KEYS, DH).astype(BF16)

        def tile(t, carry):
            limit = (
                order_ref[blk * 2 + t // 2] * 64 + (t % 2) * 32 + (z % 4 // 2) * 16
                + (lane // 128) * 8 + (lane // GROUP) % TOK
            )
            s = dot(ks[...], qt[t])
            at = pos[d]
            s = jnp.where(jnp.concatenate((at, at), axis=1) <= limit, s, -1e30)
            old = top[t]
            new = jnp.maximum(old, jnp.max(s, axis=0, keepdims=True))
            e = jnp.exp2((s - new) * RATE)
            prob[d, t] = e
            dp = dot(vs[...], gt[t])
            dprob[d, t] = dp
            fade = jnp.exp2((old - new) * RATE)
            total[t] = total[t] * fade + jnp.sum(e, axis=0, keepdims=True)
            mixed[t] = mixed[t] * fade + jnp.sum(e * dp, axis=0, keepdims=True)
            tops[d, t] = new
            top[t] = new
            return carry

        lax.fori_loop(0, TILES, tile, 0)

    visits = (0,) + Z_ORDER
    for k, d in enumerate(visits):
        if k:
            arrived(kvg.at[(zq + NQ - d) % NQ, x, c], z_s.at[d], z_r.at[d])
            share(d)
            swap(visits[k - 1])
        if k == 1:
            take_queries()
        if k >= 2:
            score(visits[k - 2])
    swap(visits[-1])
    score(visits[-2])
    score(visits[-1])
    total[...] = 1.0 / total[...]
    mixed[...] = mixed[...] * total[...]

    def grads(d):
        u = (NQ - d) % NQ
        dk[...] = jnp.zeros_like(dk)
        dv[...] = jnp.zeros_like(dv)

        def tile(t, carry):
            share_of = jnp.exp2((tops[u, t] - top[t]) * RATE) * total[t]
            p = prob[u, t] * share_of
            ds = (p * (dprob[u, t] - mixed[t])).astype(BF16)
            dv[...] += dot(p.astype(BF16), ga[pl.ds(2 * t, 2)].reshape(TR, DH))
            dk[...] += dot(ds, qa[pl.ds(2 * t, 2)].reshape(TR, DH))
            dqt[t] += dot(kt[u], ds)
            return carry

        lax.fori_loop(0, TILES, tile, 0)
        both = jnp.stack(((dk[...] * SCALE).reshape(CHUNKS, TOK, DH), dv[...].reshape(CHUNKS, TOK, DH)), axis=1)
        dkv[d] = both.reshape(NX, 2, PEERS, 16, DH).astype(BF16)
        start(dkv.at[d, :, 1 - c], cx.at[d], d_s.at[d], d_r.at[d], other)

    def along_x(d):
        arrived(cx.at[d], d_s.at[d], d_r.at[d])
        for e in X_ORDER:
            xd = (x + e) % NX
            xst[d, e] = (dkv[d, xd, c].astype(F32) + cx[d, xd].astype(F32)).astype(BF16)
            start(xst.at[d, e], xr.at[d, e], e_s.at[d, e], e_r.at[d, e], device(xd, y, z, c))

    def along_z(d):
        part = dkv[d, x, c].astype(F32) + cx[d, x].astype(F32)
        for e in X_ORDER:
            arrived(xr.at[d, e], e_s.at[d, e], e_r.at[d, e])
            part = part + xr[d, e].astype(F32)
        if d:
            zst[d] = part.astype(BF16)
            start(zst.at[d], zr.at[d], f_s.at[d], f_r.at[d], device(x, y, (z + 2 * d) % NZ, c))
        return part

    for k, d in enumerate(BACK):
        grads(d)
        if k >= 1:
            along_x(BACK[k - 1])
        if k >= 3:
            along_z(BACK[k - 3])
    along_x(BACK[-1])
    along_z(BACK[-3])
    for t in range(TILES):
        dqs[2 * t:2 * t + 2] = (dqt[t] * SCALE).T.astype(BF16).reshape(2, TOK, GROUP, DH)
    along_z(BACK[-2])
    dq_own = pltpu.make_async_copy(dqs.at[m], dqh_ref.at[:, pl.ds(m * GROUP, GROUP), :], own.at[3])
    dq_own.start()
    for d in range(1, PEERS):
        n = (m + d) % PEERS
        start(dqs.at[n], dqh_ref.at[:, pl.ds(m * GROUP, GROUP), :], o_s.at[d], o_r.at[d], peer(x, z, c, n))
    part = along_z(BACK[-1])
    for d in BACK[:-1]:
        arrived(zr.at[d], f_s.at[d], f_r.at[d])
        part = part + zr[d].astype(F32)
    fst[...] = part.astype(BF16)
    for d in range(1, PEERS):
        n = (m + d) % PEERS
        start(fst.at[n], dkvh_ref.at[m], h_s.at[d], h_r.at[d], peer(x, z, c, n))
    kv_home = pltpu.make_async_copy(fst.at[m], dkvh_ref.at[m], own.at[4])
    kv_home.start()
    dq_own.wait()
    kv_home.wait()
    for d in range(1, PEERS):
        n = (m + PEERS - d) % PEERS
        arrived(dqh_ref.at[:, pl.ds(n * GROUP, GROUP), :], o_s.at[d], o_r.at[d])
        arrived(dkvh_ref.at[n], h_s.at[d], h_r.at[d])
    for one in sends:
        one.wait_send()


def backward(order, q, g, kv):
    sem = pltpu.SemaphoreType.DMA
    hbm = pl.BlockSpec(memory_space=pl.ANY)
    vmem = pl.BlockSpec(memory_space=pltpu.VMEM)
    block = (PEERS, 16, DH)
    rows = (PEERS, TOK, GROUP, DH)
    stat = pltpu.VMEM((TILES, 1, TR), F32)
    one, two = sem((NQ,)), sem((NQ, NX))
    return pl.pallas_call(
        kernel,
        out_shape=(jax.ShapeDtypeStruct((TOK, PEERS * GROUP, DH), BF16), jax.ShapeDtypeStruct(block, BF16)),
        in_specs=[pl.BlockSpec(memory_space=pltpu.SMEM), hbm, hbm, hbm],
        out_specs=[vmem, vmem],
        scratch_shapes=[
            pltpu.VMEM(rows, BF16), pltpu.VMEM(rows, BF16),
            pltpu.VMEM((TILES, DH, TR), BF16), pltpu.VMEM((TILES, DH, TR), BF16),
            pltpu.VMEM((NQ, NX, 2) + block, BF16),
            pltpu.VMEM((KEYS, DH), BF16), pltpu.VMEM((KEYS, DH), BF16), pltpu.VMEM((NQ, DH, KEYS), BF16),
            pltpu.VMEM((NQ, KEYS, DH), jnp.int32),
            pltpu.VMEM((NQ, TILES, KEYS, TR), F32), pltpu.VMEM((NQ, TILES, KEYS, TR), F32),
            pltpu.VMEM((NQ, TILES, 1, TR), F32), stat, stat, stat,
            pltpu.VMEM((KEYS, DH), F32), pltpu.VMEM((KEYS, DH), F32),
            pltpu.VMEM((TILES, DH, TR), F32), pltpu.VMEM(rows, BF16),
            pltpu.VMEM((NQ, NX, 2) + block, BF16), pltpu.VMEM((NQ, NX) + block, BF16),
            pltpu.VMEM((NQ, NX) + block, BF16), pltpu.VMEM((NQ, NX) + block, BF16),
            pltpu.VMEM((NQ,) + block, BF16), pltpu.VMEM((NQ,) + block, BF16), pltpu.VMEM(block, BF16),
            one, one, one, one, two, two, one, one, one, one, one, one,
            one, one, two, two, one, one, one, one, one, one, sem((5,)),
        ],
        compiler_params=pltpu.CompilerParams(collective_id=0, has_side_effects=True, vmem_limit_bytes=58 << 20),
        name="attention_backward",
    )(order, q, g, kv)


def on_device(query, key, value, out_grad, block_order):
    kv = jnp.concatenate((jnp.transpose(key, (1, 0, 2)), jnp.transpose(value, (1, 0, 2))), axis=1)
    dq_home, dkv_home = backward(block_order, query, out_grad, kv)
    grads = jnp.transpose(dkv_home, (1, 0, 2))
    return dq_home, grads[:TOK], grads[TOK:]


def solution(mesh):
    rows = P(("blk", "head"), None, None)
    return jax.shard_map(
        on_device, mesh=mesh, in_specs=(rows,) * 4 + (P(),), out_specs=(rows,) * 3, check_vma=False
    )
```

```python
import math

import jax
import jax.numpy as jnp
from jax import lax
from jax.experimental import pallas as pl
from jax.experimental.pallas import tpu as pltpu
from jax.sharding import PartitionSpec as P

MESH = pl.DeviceIdType.MESH
F32 = jnp.float32
BF16 = jnp.bfloat16
NX, NY, NZ = 4, 4, 16
PLANE = NX * NY
HEADS = 8
TOK = 8
GROUP = 16
DH = 128
TILES = 4
TR = HEADS * TOK * GROUP // TILES
CHUNKS = 2 * NZ
KEYS = CHUNKS * TOK
SCALE = DH ** -0.5
RATE = SCALE * math.log2(math.e)
PAIRS = ((1, 3), (4, 12), (5, 15), (7, 13), (2, 8), (6, 14), (9, 11), (0, 10))
UNITS = len(PAIRS)
NEAR = tuple(d for pair in PAIRS for d in pair if d)


def opposite(d):
    return (NX - d // NY) % NX * NY + (NY - d % NY) % NY


def place():
    blk = lax.axis_index("blk")
    head = lax.axis_index("head")
    z = (blk // 8) * 4 + head % 4
    return (blk // 2) % 4, head // 4, z, blk % 2


def device(x, y, z, c):
    return (((z // 4) * 4 + x) * 2 + c, y * 4 + z % 4)


def turn(o, z):
    return 8 * ((o + 3) // 8) + 8 * (z % 2) * (o // 4 - (o + 3) // 8)


def given_to(o, z):
    return (z + o + turn(o, z)) % NZ


def got_from(o, z):
    return (z + NZ - o + turn(o, z)) % NZ


def dot(a, b):
    return lax.dot_general(a, b, (((1,), (0,)), ((), ())), preferred_element_type=F32)


def kernel(
    order_ref, q_ref, k_ref, v_ref, g_ref, dqh_ref, dkh_ref, dvh_ref,
    kin, vin, kv, qa, ga, qt, gt, kvg, ks, vs, kt, pos, prob, dprob, tops, top, total, mixed, dk, dv, dqt, dqs,
    dkv, cx, pst, pr, fst, fin,
    k_s, k_r, p_s, p_r, c_s, c_r, q_s, q_r, g_s, g_r, d_s, d_r, e_s, e_r, f_s, f_r, o_s, o_r, own,
):
    x, y, z, c = place()
    i = x * NY + y
    head = z % HEADS
    other = device(x, y, z, 1 - c)
    sends = []

    def copy(src, dst, ss, rs, to):
        return pltpu.make_async_remote_copy(
            src_ref=src, dst_ref=dst, send_sem=ss, recv_sem=rs, device_id=to, device_id_type=MESH
        )

    def start(src, dst, ss, rs, to):
        one = copy(src, dst, ss, rs, to)
        one.start()
        sends.append(one)

    def arrived(dst, ss, rs):
        copy(dst, dst, ss, rs, other).wait_recv()

    def local(src, dst, at):
        one = pltpu.make_async_copy(src, dst, own.at[at])
        one.start()
        return one

    def away(d):
        return device((x + d // NY) % NX, (y + d % NY) % NY, z, c)

    def source(d):
        return (x + NX - d // NY) % NX * NY + (y + NY - d % NY) % NY

    barrier = pltpu.get_barrier_semaphore()
    to = [device(x, y, (z + d) % NZ, c) for d in range(1, NZ)]
    to += [away(d) for d in range(1, PLANE)]
    to += [other]
    for one in to:
        pl.semaphore_signal(barrier, inc=1, device_id=one, device_id_type=MESH)

    k_in = local(k_ref, kin, 0)
    v_in = local(v_ref, vin, 1)
    q_own = local(q_ref.at[:, pl.ds(head * GROUP, GROUP), :], qa.at[0], 2)
    g_own = local(g_ref.at[:, pl.ds(head * GROUP, GROUP), :], ga.at[0], 3)
    k_in.wait()
    v_in.wait()
    kv[...] = jnp.concatenate(
        (jnp.swapaxes(kin[...].astype(F32), 0, 1), jnp.swapaxes(vin[...].astype(F32), 0, 1)), axis=1
    ).astype(BF16)
    kv_own = local(kv.at[head], kvg.at[i, c, z], 4)

    step = lax.broadcasted_iota(jnp.int32, (TOK, DH), 0)

    def place_keys(d, carry):
        xs = (x + NX - d // NY) % NX
        ys = (y + NY - d % NY) % NY
        for cc in range(2):
            for zz in range(NZ):
                first = order_ref[(zz // 4) * 16 + xs * 4 + cc * 2 + ys // 2] * 64 + (ys % 2) * 32 + (zz % 4) * 8
                at = (cc * NZ + zz) * TOK
                pos[d, at:at + TOK, :] = first + step
        return carry

    lax.fori_loop(0, PLANE, place_keys, 0)
    top[...] = jnp.full_like(top, -1e30)
    total[...] = jnp.zeros_like(total)
    mixed[...] = jnp.zeros_like(mixed)
    dqt[...] = jnp.zeros_like(dqt)
    pl.semaphore_wait(barrier, len(to))

    for d in range(1, NZ):
        zd = (z + d) % NZ
        start(kv.at[zd % HEADS], kvg.at[i, c, z], k_s.at[d], k_r.at[d], device(x, y, zd, c))
    kv_own.wait()
    for d in range(1, NZ):
        arrived(kvg.at[i, c, (z + NZ - d) % NZ], k_s.at[d], k_r.at[d])
    for d in NEAR:
        start(kvg.at[i, c], kvg.at[i, c], p_s.at[d], p_r.at[d], away(d))
    start(kvg.at[i, c], kvg.at[i, c], c_s.at[0], c_r.at[0], other)
    for o in range(1, HEADS):
        zd = given_to(o, z)
        rows = pl.ds(zd % HEADS * GROUP, GROUP)
        start(q_ref.at[:, rows, :], qa.at[o], q_s.at[o], q_r.at[o], device(x, y, zd, c))
        start(g_ref.at[:, rows, :], ga.at[o], g_s.at[o], g_r.at[o], device(x, y, zd, c))

    lane = lax.broadcasted_iota(jnp.int32, (1, TR), 1)

    def take_queries():
        q_own.wait()
        g_own.wait()
        for o in range(1, HEADS):
            arrived(qa.at[o], q_s.at[o], q_r.at[o])
            arrived(ga.at[o], g_s.at[o], g_r.at[o])
        for t in range(TILES):
            qt[t] = qa[2 * t:2 * t + 2].reshape(TR, DH).T
            gt[t] = ga[2 * t:2 * t + 2].reshape(TR, DH).T

    def swap(d):
        if d:
            p = source(d)
            arrived(kvg.at[p, c], p_s.at[d], p_r.at[d])
            start(kvg.at[p, c], kvg.at[p, c], c_s.at[d], c_r.at[d], other)

    def score(u):
        for j, d in enumerate(PAIRS[u]):
            p = source(d)
            arrived(kvg.at[p, 1 - c], c_s.at[d], c_r.at[d])
            both = kvg[p].reshape(CHUNKS, 16, DH).astype(F32).reshape(CHUNKS, 2, TOK, DH)
            k = both[:, 0].reshape(KEYS, DH).astype(BF16)
            ks[j * KEYS:(j + 1) * KEYS, :] = k
            kt[u, :, j * KEYS:(j + 1) * KEYS] = k.T
            vs[j * KEYS:(j + 1) * KEYS, :] = both[:, 1].reshape(KEYS, DH).astype(BF16)

        def tile(t, carry):
            limit = (lane // GROUP) % TOK + (y % 2) * 32
            for j in range(2):
                zs = got_from(2 * t + j, z)
                first = order_ref[(zs // 4) * 16 + x * 4 + c * 2 + y // 2] * 64 + (zs % 4) * 8
                limit = limit + jnp.where(lane // DH == j, first, 0)
            s = dot(ks[...], qt[t])
            at = jnp.concatenate((pos[PAIRS[u][0]], pos[PAIRS[u][1]]), axis=0)
            s = jnp.where(jnp.concatenate((at, at), axis=1) <= limit, s, -1e30)
            old = top[t]
            new = jnp.maximum(old, jnp.max(s, axis=0, keepdims=True))
            e = jnp.exp2((s - new) * RATE)
            prob[u, t] = e
            dp = dot(vs[...], gt[t])
            dprob[u, t] = dp
            fade = jnp.exp2((old - new) * RATE)
            total[t] = total[t] * fade + jnp.sum(e, axis=0, keepdims=True)
            mixed[t] = mixed[t] * fade + jnp.sum(e * dp, axis=0, keepdims=True)
            tops[u, t] = new
            top[t] = new
            return carry

        lax.fori_loop(0, TILES, tile, 0)

    for u in range(UNITS):
        for d in PAIRS[u]:
            swap(d)
        if u == 1:
            take_queries()
        if u >= 1:
            score(u - 1)
    score(UNITS - 1)
    total[...] = 1.0 / total[...]
    mixed[...] = mixed[...] * total[...]

    def grads(u):
        dk[...] = jnp.zeros_like(dk)
        dv[...] = jnp.zeros_like(dv)

        def tile(t, carry):
            share_of = jnp.exp2((tops[u, t] - top[t]) * RATE) * total[t]
            p = prob[u, t] * share_of
            ds = (p * (dprob[u, t] - mixed[t])).astype(BF16)
            dv[...] += dot(p.astype(BF16), ga[pl.ds(2 * t, 2)].reshape(TR, DH))
            dk[...] += dot(ds, qa[pl.ds(2 * t, 2)].reshape(TR, DH))
            dqt[t] += dot(kt[u], ds)
            return carry

        lax.fori_loop(0, TILES, tile, 0)
        for j, d in enumerate(PAIRS[u]):
            rows = slice(j * KEYS, (j + 1) * KEYS)
            both = jnp.stack(((dk[rows, :] * SCALE).reshape(CHUNKS, TOK, DH), dv[rows, :].reshape(CHUNKS, TOK, DH)), axis=1)
            dkv[d] = both.reshape(2, NZ, 16, DH).astype(BF16)
            start(dkv.at[d, 1 - c], cx.at[d], d_s.at[d], d_r.at[d], other)

    def along(u):
        for d in PAIRS[u]:
            arrived(cx.at[d], d_s.at[d], d_r.at[d])
            if d:
                back = opposite(d)
                pst[d] = (dkv[d, c].astype(F32) + cx[d].astype(F32)).astype(BF16)
                start(pst.at[d], pr.at[back], e_s.at[back], e_r.at[back], away(back))

    late = tuple(reversed(range(UNITS)))
    for k, u in enumerate(late):
        grads(u)
        if k:
            along(late[k - 1])
    along(late[-1])
    for t in range(TILES):
        dqs[2 * t:2 * t + 2] = (dqt[t] * SCALE).T.astype(BF16).reshape(2, TOK, GROUP, DH)
    rows = pl.ds(head * GROUP, GROUP)
    dq_own = local(dqs.at[0], dqh_ref.at[:, rows, :], 2)
    for o in range(1, HEADS):
        start(dqs.at[o], dqh_ref.at[:, rows, :], o_s.at[o], o_r.at[o], device(x, y, got_from(o, z), c))
    part = dkv[0, c].astype(F32) + cx[0].astype(F32)
    for u in late:
        for d in PAIRS[u]:
            if d:
                arrived(pr.at[d], e_s.at[d], e_r.at[d])
                part = part + pr[d].astype(F32)
    fst[...] = part.astype(BF16)
    for d in range(1, NZ):
        zd = (z + d) % NZ
        start(fst.at[zd], fin.at[z], f_s.at[d], f_r.at[d], device(x, y, zd, c))
    kv_home = local(fst.at[z], fin.at[z], 4)
    kv_home.wait()
    for d in range(1, NZ):
        arrived(fin.at[(z + NZ - d) % NZ], f_s.at[d], f_r.at[d])
    home = fin[:HEADS].astype(F32) + fin[HEADS:].astype(F32)
    dkh_ref[...] = jnp.swapaxes(home[:, :TOK], 0, 1).astype(BF16)
    dvh_ref[...] = jnp.swapaxes(home[:, TOK:], 0, 1).astype(BF16)
    dq_own.wait()
    for o in range(1, HEADS):
        arrived(dqh_ref.at[:, pl.ds(given_to(o, z) % HEADS * GROUP, GROUP), :], o_s.at[o], o_r.at[o])
    for one in sends:
        one.wait_send()


def backward(order, query, key, value, out_grad):
    sem = pltpu.SemaphoreType.DMA
    hbm = pl.BlockSpec(memory_space=pl.ANY)
    vmem = pl.BlockSpec(memory_space=pltpu.VMEM)
    block = (NZ, 16, DH)
    rows = (HEADS, TOK, GROUP, DH)
    home = (TOK, HEADS, DH)
    stat = pltpu.VMEM((TILES, 1, TR), F32)
    eight, many = sem((HEADS,)), sem((NZ,))
    return pl.pallas_call(
        kernel,
        out_shape=(
            jax.ShapeDtypeStruct((TOK, HEADS * GROUP, DH), BF16),
            jax.ShapeDtypeStruct(home, BF16),
            jax.ShapeDtypeStruct(home, BF16),
        ),
        in_specs=[pl.BlockSpec(memory_space=pltpu.SMEM), hbm, hbm, hbm, hbm],
        out_specs=[vmem, vmem, vmem],
        scratch_shapes=[
            pltpu.VMEM(home, BF16), pltpu.VMEM(home, BF16), pltpu.VMEM((HEADS, 16, DH), BF16),
            pltpu.VMEM(rows, BF16), pltpu.VMEM(rows, BF16),
            pltpu.VMEM((TILES, DH, TR), BF16), pltpu.VMEM((TILES, DH, TR), BF16),
            pltpu.VMEM((PLANE, 2) + block, BF16),
            pltpu.VMEM((2 * KEYS, DH), BF16), pltpu.VMEM((2 * KEYS, DH), BF16), pltpu.VMEM((UNITS, DH, 2 * KEYS), BF16),
            pltpu.VMEM((PLANE, KEYS, DH), jnp.int32),
            pltpu.VMEM((UNITS, TILES, 2 * KEYS, TR), F32), pltpu.VMEM((UNITS, TILES, 2 * KEYS, TR), F32),
            pltpu.VMEM((UNITS, TILES, 1, TR), F32), stat, stat, stat,
            pltpu.VMEM((2 * KEYS, DH), F32), pltpu.VMEM((2 * KEYS, DH), F32),
            pltpu.VMEM((TILES, DH, TR), F32), pltpu.VMEM(rows, BF16),
            pltpu.VMEM((PLANE, 2) + block, BF16), pltpu.VMEM((PLANE,) + block, BF16),
            pltpu.VMEM((PLANE,) + block, BF16), pltpu.VMEM((PLANE,) + block, BF16),
            pltpu.VMEM(block, BF16), pltpu.VMEM(block, BF16),
            many, many, many, many, many, many, eight, eight, eight, eight,
            many, many, many, many, many, many, eight, eight, sem((5,)),
        ],
        compiler_params=pltpu.CompilerParams(collective_id=0, has_side_effects=True, vmem_limit_bytes=58 << 20),
        name="attention_backward",
    )(order, query, key, value, out_grad)


def on_device(query, key, value, out_grad, block_order):
    return backward(block_order, query, key, value, out_grad)


def solution(mesh):
    rows = P(("blk", "head"), None, None)
    return jax.shard_map(
        on_device, mesh=mesh, in_specs=(rows,) * 4 + (P(),), out_specs=(rows,) * 3, check_vma=False
    )
```

```python
import math

import jax
import jax.numpy as jnp
from jax import lax
from jax.experimental import pallas as pl
from jax.experimental.pallas import tpu as pltpu
from jax.sharding import PartitionSpec as P

MESH = pl.DeviceIdType.MESH
F32 = jnp.float32
BF16 = jnp.bfloat16
NX, NY, NZ = 4, 4, 16
PLANE = NX * NY
HEADS = 8
TOK = 8
GROUP = 16
DH = 128
TILES = 4
TR = HEADS * TOK * GROUP // TILES
CHUNKS = 2 * NZ
KEYS = CHUNKS * TOK
SCALE = DH ** -0.5
RATE = SCALE * math.log2(math.e)
PAIRS = ((1, 3), (4, 12), (5, 15), (7, 13), (2, 8), (6, 14), (9, 11), (0, 10))
UNITS = len(PAIRS)
NEAR = tuple(d for pair in PAIRS for d in pair if d)


def opposite(d):
    return (NX - d // NY) % NX * NY + (NY - d % NY) % NY


def place():
    blk = lax.axis_index("blk")
    head = lax.axis_index("head")
    z = (blk // 8) * 4 + head % 4
    return (blk // 2) % 4, head // 4, z, blk % 2


def device(x, y, z, c):
    return (((z // 4) * 4 + x) * 2 + c, y * 4 + z % 4)


def turn(o, z):
    return 8 * ((o + 3) // 8) + 8 * (z % 2) * (o // 4 - (o + 3) // 8)


def given_to(o, z):
    return (z + o + turn(o, z)) % NZ


def got_from(o, z):
    return (z + NZ - o + turn(o, z)) % NZ


def dot(a, b):
    return lax.dot_general(a, b, (((1,), (0,)), ((), ())), preferred_element_type=F32)


def kernel(
    order_ref, q_ref, k_ref, v_ref, g_ref, dqh_ref, dkh_ref, dvh_ref,
    kin, vin, kv, qa, ga, qt, gt, kvg, ks, vs, kt, pos, prob, dprob, tops, top, total, mixed, dk, dv, dqt, dqs,
    dkv, cx, pst, pr, fst, fin,
    k_s, k_r, p_s, p_r, c_s, c_r, q_s, q_r, g_s, g_r, d_s, d_r, e_s, e_r, f_s, f_r, o_s, o_r, own,
):
    x, y, z, c = place()
    i = x * NY + y
    head = z % HEADS
    other = device(x, y, z, 1 - c)
    sends = []

    def copy(src, dst, ss, rs, to):
        return pltpu.make_async_remote_copy(
            src_ref=src, dst_ref=dst, send_sem=ss, recv_sem=rs, device_id=to, device_id_type=MESH
        )

    def start(src, dst, ss, rs, to):
        one = copy(src, dst, ss, rs, to)
        one.start()
        sends.append(one)

    def arrived(dst, ss, rs):
        copy(dst, dst, ss, rs, other).wait_recv()

    def local(src, dst, at):
        one = pltpu.make_async_copy(src, dst, own.at[at])
        one.start()
        return one

    def away(d):
        return device((x + d // NY) % NX, (y + d % NY) % NY, z, c)

    def source(d):
        return (x + NX - d // NY) % NX * NY + (y + NY - d % NY) % NY

    barrier = pltpu.get_barrier_semaphore()
    to = [device(x, y, (z + d) % NZ, c) for d in range(1, NZ)]
    to += [away(d) for d in range(1, PLANE)]
    to += [other]
    for one in to:
        pl.semaphore_signal(barrier, inc=1, device_id=one, device_id_type=MESH)

    k_in = local(k_ref, kin, 0)
    v_in = local(v_ref, vin, 1)
    q_own = local(q_ref.at[:, pl.ds(head * GROUP, GROUP), :], qa.at[0], 2)
    g_own = local(g_ref.at[:, pl.ds(head * GROUP, GROUP), :], ga.at[0], 3)
    k_in.wait()
    v_in.wait()
    kv[...] = jnp.concatenate(
        (jnp.swapaxes(kin[...].astype(F32), 0, 1), jnp.swapaxes(vin[...].astype(F32), 0, 1)), axis=1
    ).astype(BF16)
    kv_own = local(kv.at[head], kvg.at[i, c, z], 4)

    step = lax.broadcasted_iota(jnp.int32, (TOK, DH), 0)

    def place_keys(d, carry):
        xs = (x + NX - d // NY) % NX
        ys = (y + NY - d % NY) % NY
        for cc in range(2):
            for zz in range(NZ):
                first = order_ref[(zz // 4) * 16 + xs * 4 + cc * 2 + ys // 2] * 64 + (ys % 2) * 32 + (zz % 4) * 8
                at = (cc * NZ + zz) * TOK
                pos[d, at:at + TOK, :] = first + step
        return carry

    lax.fori_loop(0, PLANE, place_keys, 0)
    top[...] = jnp.full_like(top, -1e30)
    total[...] = jnp.zeros_like(total)
    mixed[...] = jnp.zeros_like(mixed)
    dqt[...] = jnp.zeros_like(dqt)
    pl.semaphore_wait(barrier, len(to))

    for d in range(1, NZ):
        zd = (z + d) % NZ
        start(kv.at[zd % HEADS], kvg.at[i, c, z], k_s.at[d], k_r.at[d], device(x, y, zd, c))
    for o in range(1, HEADS):
        zd = given_to(o, z)
        rows = pl.ds(zd % HEADS * GROUP, GROUP)
        start(q_ref.at[:, rows, :], qa.at[o], q_s.at[o], q_r.at[o], device(x, y, zd, c))
        start(g_ref.at[:, rows, :], ga.at[o], g_s.at[o], g_r.at[o], device(x, y, zd, c))
    kv_own.wait()
    for d in range(1, NZ):
        arrived(kvg.at[i, c, (z + NZ - d) % NZ], k_s.at[d], k_r.at[d])
    def spread(u):
        for d in PAIRS[u]:
            if d:
                start(kvg.at[i, c], kvg.at[i, c], p_s.at[d], p_r.at[d], away(d))

    for u in range(3):
        spread(u)
    start(kvg.at[i, c], kvg.at[i, c], c_s.at[0], c_r.at[0], other)

    lane = lax.broadcasted_iota(jnp.int32, (1, TR), 1)

    def take_queries():
        q_own.wait()
        g_own.wait()
        for o in range(1, HEADS):
            arrived(qa.at[o], q_s.at[o], q_r.at[o])
            arrived(ga.at[o], g_s.at[o], g_r.at[o])
        for t in range(TILES):
            qt[t] = qa[2 * t:2 * t + 2].reshape(TR, DH).T
            gt[t] = ga[2 * t:2 * t + 2].reshape(TR, DH).T

    def swap(d):
        if d:
            p = source(d)
            arrived(kvg.at[p, c], p_s.at[d], p_r.at[d])
            start(kvg.at[p, c], kvg.at[p, c], c_s.at[d], c_r.at[d], other)

    def score(u):
        for j, d in enumerate(PAIRS[u]):
            p = source(d)
            arrived(kvg.at[p, 1 - c], c_s.at[d], c_r.at[d])
            both = kvg[p].reshape(CHUNKS, 16, DH).astype(F32).reshape(CHUNKS, 2, TOK, DH)
            k = both[:, 0].reshape(KEYS, DH).astype(BF16)
            ks[j * KEYS:(j + 1) * KEYS, :] = k
            kt[u, :, j * KEYS:(j + 1) * KEYS] = k.T
            vs[j * KEYS:(j + 1) * KEYS, :] = both[:, 1].reshape(KEYS, DH).astype(BF16)

        def tile(t, carry):
            limit = (lane // GROUP) % TOK + (y % 2) * 32
            for j in range(2):
                zs = got_from(2 * t + j, z)
                first = order_ref[(zs // 4) * 16 + x * 4 + c * 2 + y // 2] * 64 + (zs % 4) * 8
                limit = limit + jnp.where(lane // DH == j, first, 0)
            s = dot(ks[...], qt[t])
            at = jnp.concatenate((pos[PAIRS[u][0]], pos[PAIRS[u][1]]), axis=0)
            s = jnp.where(jnp.concatenate((at, at), axis=1) <= limit, s, -1e30)
            old = top[t]
            new = jnp.maximum(old, jnp.max(s, axis=0, keepdims=True))
            e = jnp.exp2((s - new) * RATE)
            prob[u, t] = e
            dp = dot(vs[...], gt[t])
            dprob[u, t] = dp
            fade = jnp.exp2((old - new) * RATE)
            total[t] = total[t] * fade + jnp.sum(e, axis=0, keepdims=True)
            mixed[t] = mixed[t] * fade + jnp.sum(e * dp, axis=0, keepdims=True)
            tops[u, t] = new
            top[t] = new
            return carry

        lax.fori_loop(0, TILES, tile, 0, unroll=4)

    for u in range(UNITS):
        for d in PAIRS[u]:
            swap(d)
        if u + 3 < UNITS:
            spread(u + 3)
        if u == 1:
            take_queries()
        if u >= 1:
            score(u - 1)
    score(UNITS - 1)
    total[...] = 1.0 / total[...]
    mixed[...] = mixed[...] * total[...]

    def grads(u):
        dk[...] = jnp.zeros_like(dk)
        dv[...] = jnp.zeros_like(dv)

        def tile(t, carry):
            share_of = jnp.exp2((tops[u, t] - top[t]) * RATE) * total[t]
            p = prob[u, t] * share_of
            ds = (p * (dprob[u, t] - mixed[t])).astype(BF16)
            dv[...] += dot(p.astype(BF16), ga[pl.ds(2 * t, 2)].reshape(TR, DH))
            dk[...] += dot(ds, qa[pl.ds(2 * t, 2)].reshape(TR, DH))
            dqt[t] += dot(kt[u], ds)
            return carry

        lax.fori_loop(0, TILES, tile, 0, unroll=4)
        for j, d in enumerate(PAIRS[u]):
            rows = slice(j * KEYS, (j + 1) * KEYS)
            both = jnp.stack(((dk[rows, :] * SCALE).reshape(CHUNKS, TOK, DH), dv[rows, :].reshape(CHUNKS, TOK, DH)), axis=1)
            dkv[d] = both.reshape(2, NZ, 16, DH).astype(BF16)
            start(dkv.at[d, 1 - c], cx.at[d], d_s.at[d], d_r.at[d], other)

    def along(u):
        for d in PAIRS[u]:
            arrived(cx.at[d], d_s.at[d], d_r.at[d])
            if d:
                back = opposite(d)
                pst[d] = (dkv[d, c].astype(F32) + cx[d].astype(F32)).astype(BF16)
                start(pst.at[d], pr.at[back], e_s.at[back], e_r.at[back], away(back))

    late = tuple(reversed(range(UNITS)))
    for k, u in enumerate(late):
        grads(u)
        if k:
            along(late[k - 1])
    along(late[-1])
    for t in range(TILES):
        dqs[2 * t:2 * t + 2] = (dqt[t] * SCALE).T.astype(BF16).reshape(2, TOK, GROUP, DH)
    rows = pl.ds(head * GROUP, GROUP)
    dq_own = local(dqs.at[0], dqh_ref.at[:, rows, :], 2)
    for o in range(1, HEADS):
        start(dqs.at[o], dqh_ref.at[:, rows, :], o_s.at[o], o_r.at[o], device(x, y, got_from(o, z), c))
    part = dkv[0, c].astype(F32) + cx[0].astype(F32)
    for u in late:
        for d in PAIRS[u]:
            if d:
                arrived(pr.at[d], e_s.at[d], e_r.at[d])
                part = part + pr[d].astype(F32)
    fst[...] = part.astype(BF16)
    for d in range(1, NZ):
        zd = (z + d) % NZ
        start(fst.at[zd], fin.at[z], f_s.at[d], f_r.at[d], device(x, y, zd, c))
    kv_home = local(fst.at[z], fin.at[z], 4)
    kv_home.wait()
    for d in range(1, NZ):
        arrived(fin.at[(z + NZ - d) % NZ], f_s.at[d], f_r.at[d])
    home = fin[:HEADS].astype(F32) + fin[HEADS:].astype(F32)
    dkh_ref[...] = jnp.swapaxes(home[:, :TOK], 0, 1).astype(BF16)
    dvh_ref[...] = jnp.swapaxes(home[:, TOK:], 0, 1).astype(BF16)
    dq_own.wait()
    for o in range(1, HEADS):
        arrived(dqh_ref.at[:, pl.ds(given_to(o, z) % HEADS * GROUP, GROUP), :], o_s.at[o], o_r.at[o])
    for one in sends:
        one.wait_send()


def backward(order, query, key, value, out_grad):
    sem = pltpu.SemaphoreType.DMA
    hbm = pl.BlockSpec(memory_space=pl.ANY)
    vmem = pl.BlockSpec(memory_space=pltpu.VMEM)
    block = (NZ, 16, DH)
    rows = (HEADS, TOK, GROUP, DH)
    home = (TOK, HEADS, DH)
    stat = pltpu.VMEM((TILES, 1, TR), F32)
    eight, many = sem((HEADS,)), sem((NZ,))
    return pl.pallas_call(
        kernel,
        out_shape=(
            jax.ShapeDtypeStruct((TOK, HEADS * GROUP, DH), BF16),
            jax.ShapeDtypeStruct(home, BF16),
            jax.ShapeDtypeStruct(home, BF16),
        ),
        in_specs=[pl.BlockSpec(memory_space=pltpu.SMEM), hbm, hbm, hbm, hbm],
        out_specs=[vmem, vmem, vmem],
        scratch_shapes=[
            pltpu.VMEM(home, BF16), pltpu.VMEM(home, BF16), pltpu.VMEM((HEADS, 16, DH), BF16),
            pltpu.VMEM(rows, BF16), pltpu.VMEM(rows, BF16),
            pltpu.VMEM((TILES, DH, TR), BF16), pltpu.VMEM((TILES, DH, TR), BF16),
            pltpu.VMEM((PLANE, 2) + block, BF16),
            pltpu.VMEM((2 * KEYS, DH), BF16), pltpu.VMEM((2 * KEYS, DH), BF16), pltpu.VMEM((UNITS, DH, 2 * KEYS), BF16),
            pltpu.VMEM((PLANE, KEYS, DH), jnp.int32),
            pltpu.VMEM((UNITS, TILES, 2 * KEYS, TR), F32), pltpu.VMEM((UNITS, TILES, 2 * KEYS, TR), F32),
            pltpu.VMEM((UNITS, TILES, 1, TR), F32), stat, stat, stat,
            pltpu.VMEM((2 * KEYS, DH), F32), pltpu.VMEM((2 * KEYS, DH), F32),
            pltpu.VMEM((TILES, DH, TR), F32), pltpu.VMEM(rows, BF16),
            pltpu.VMEM((PLANE, 2) + block, BF16), pltpu.VMEM((PLANE,) + block, BF16),
            pltpu.VMEM((PLANE,) + block, BF16), pltpu.VMEM((PLANE,) + block, BF16),
            pltpu.VMEM(block, BF16), pltpu.VMEM(block, BF16),
            many, many, many, many, many, many, eight, eight, eight, eight,
            many, many, many, many, many, many, eight, eight, sem((5,)),
        ],
        compiler_params=pltpu.CompilerParams(collective_id=0, has_side_effects=True, vmem_limit_bytes=58 << 20),
        name="attention_backward",
    )(order, query, key, value, out_grad)


def on_device(query, key, value, out_grad, block_order):
    return backward(block_order, query, key, value, out_grad)


def solution(mesh):
    rows = P(("blk", "head"), None, None)
    return jax.shard_map(
        on_device, mesh=mesh, in_specs=(rows,) * 4 + (P(),), out_specs=(rows,) * 3, check_vma=False
    )
```

```python
import math

import jax
import jax.numpy as jnp
from jax import lax
from jax.experimental import pallas as pl
from jax.experimental.pallas import tpu as pltpu
from jax.sharding import PartitionSpec as P

MESH = pl.DeviceIdType.MESH
F32 = jnp.float32
BF16 = jnp.bfloat16
NX, NY, NZ = 4, 4, 16
PLANE = NX * NY
HEADS = 8
TOK = 8
GROUP = 16
DH = 128
TILES = 4
TR = HEADS * TOK * GROUP // TILES
CHUNKS = 2 * NZ
KEYS = CHUNKS * TOK
SCALE = DH ** -0.5
RATE = SCALE * math.log2(math.e)
PAIRS = ((1, 3), (4, 12), (5, 15), (7, 13), (2, 8), (6, 14), (9, 11), (0, 10))
UNITS = len(PAIRS)
HERE = 4
HALF = NZ // 2
OUTWARD = (1, 15, 2, 14, 3, 13, 4, 12, 5, 11, 6, 10, 7, 9, 8)
NEAR = tuple(d for pair in PAIRS for d in pair if d)


def opposite(d):
    return (NX - d // NY) % NX * NY + (NY - d % NY) % NY


def place():
    blk = lax.axis_index("blk")
    head = lax.axis_index("head")
    z = (blk // 8) * 4 + head % 4
    return (blk // 2) % 4, head // 4, z, blk % 2


def device(x, y, z, c):
    return (((z // 4) * 4 + x) * 2 + c, y * 4 + z % 4)


def turn(o, z):
    return 8 * ((o + 3) // 8) + 8 * (z % 2) * (o // 4 - (o + 3) // 8)


def given_to(o, z):
    return (z + o + turn(o, z)) % NZ


def got_from(o, z):
    return (z + NZ - o + turn(o, z)) % NZ


def dot(a, b):
    return lax.dot_general(a, b, (((1,), (0,)), ((), ())), preferred_element_type=F32)


def kernel(
    order_ref, q_ref, k_ref, v_ref, g_ref, dqh_ref, dkh_ref, dvh_ref,
    kin, vin, kv, qa, ga, qt, gt, kvg, ks, vs, kt, pos, prob, dprob, tops, top, total, mixed, dk, dv, dqt, dqs,
    dkv, cx, pst, pr, fst, fin,
    k_s, k_r, p_s, p_r, c_s, c_r, q_s, q_r, g_s, g_r, d_s, d_r, e_s, e_r, f_s, f_r, o_s, o_r, own,
):
    x, y, z, c = place()
    i = x * NY + y
    head = z % HEADS
    other = device(x, y, z, 1 - c)
    sends = []

    def copy(src, dst, ss, rs, to):
        return pltpu.make_async_remote_copy(
            src_ref=src, dst_ref=dst, send_sem=ss, recv_sem=rs, device_id=to, device_id_type=MESH
        )

    def start(src, dst, ss, rs, to):
        one = copy(src, dst, ss, rs, to)
        one.start()
        sends.append(one)

    def arrived(dst, ss, rs):
        copy(dst, dst, ss, rs, other).wait_recv()

    def local(src, dst, at):
        one = pltpu.make_async_copy(src, dst, own.at[at])
        one.start()
        return one

    def away(d):
        return device((x + d // NY) % NX, (y + d % NY) % NY, z, c)

    def source(d):
        return (x + NX - d // NY) % NX * NY + (y + NY - d % NY) % NY

    barrier = pltpu.get_barrier_semaphore()
    to = [device(x, y, (z + d) % NZ, c) for d in range(1, NZ)]
    to += [away(d) for d in range(1, PLANE)]
    to += [other]
    for one in to:
        pl.semaphore_signal(barrier, inc=1, device_id=one, device_id_type=MESH)

    k_in = local(k_ref, kin, 0)
    v_in = local(v_ref, vin, 1)
    q_own = local(q_ref.at[:, pl.ds(head * GROUP, GROUP), :], qa.at[0], 2)
    g_own = local(g_ref.at[:, pl.ds(head * GROUP, GROUP), :], ga.at[0], 3)
    k_in.wait()
    v_in.wait()
    kv[...] = jnp.concatenate(
        (jnp.swapaxes(kin[...].astype(F32), 0, 1), jnp.swapaxes(vin[...].astype(F32), 0, 1)), axis=1
    ).astype(BF16)
    kv_own = local(kv.at[head], kvg.at[i, c, HERE], 4)

    pl.semaphore_wait(barrier, len(to))

    for d in OUTWARD:
        zd = (z + d) % NZ
        start(kv.at[zd % HEADS], kvg.at[i, c, (HERE - d) % NZ], k_s.at[d], k_r.at[d], device(x, y, zd, c))
    for o in range(1, HEADS):
        zd = given_to(o, z)
        rows = pl.ds(zd % HEADS * GROUP, GROUP)
        start(q_ref.at[:, rows, :], qa.at[o], q_s.at[o], q_r.at[o], device(x, y, zd, c))
        start(g_ref.at[:, rows, :], ga.at[o], g_s.at[o], g_r.at[o], device(x, y, zd, c))

    step = lax.broadcasted_iota(jnp.int32, (TOK, DH), 0)

    def place_keys(d, carry):
        xs = (x + NX - d // NY) % NX
        ys = (y + NY - d % NY) % NY
        for cc in range(2):
            for zz in range(NZ):
                zs = (z + NZ + zz - HERE) % NZ
                first = order_ref[(zs // 4) * 16 + xs * 4 + cc * 2 + ys // 2] * 64 + (ys % 2) * 32 + (zs % 4) * 8
                at = (cc * NZ + zz) * TOK
                pos[d, at:at + TOK, :] = first + step
        return carry

    lax.fori_loop(0, PLANE, place_keys, 0)
    top[...] = jnp.full_like(top, -1e30)
    total[...] = jnp.zeros_like(total)
    mixed[...] = jnp.zeros_like(mixed)
    dqt[...] = jnp.zeros_like(dqt)

    kv_own.wait()
    for part, slots in enumerate((pl.ds(0, HALF), pl.ds(HALF, HALF))):
        for d in OUTWARD:
            if (HERE - d) % NZ // HALF == part:
                arrived(kvg.at[i, c, (HERE - d) % NZ], k_s.at[d], k_r.at[d])
        for d in NEAR:
            block = kvg.at[i, c, slots]
            start(block, block, p_s.at[part, d], p_r.at[part, d], away(d))
    start(kvg.at[i, c], kvg.at[i, c], c_s.at[0], c_r.at[0], other)

    lane = lax.broadcasted_iota(jnp.int32, (1, TR), 1)

    def take_queries():
        q_own.wait()
        g_own.wait()
        for o in range(1, HEADS):
            arrived(qa.at[o], q_s.at[o], q_r.at[o])
            arrived(ga.at[o], g_s.at[o], g_r.at[o])
        for t in range(TILES):
            qt[t] = qa[2 * t:2 * t + 2].reshape(TR, DH).T
            gt[t] = ga[2 * t:2 * t + 2].reshape(TR, DH).T

    def swap(d):
        if d:
            p = source(d)
            for part in range(2):
                arrived(kvg.at[p, c, pl.ds(part * HALF, HALF)], p_s.at[part, d], p_r.at[part, d])
            start(kvg.at[p, c], kvg.at[p, c], c_s.at[d], c_r.at[d], other)

    def score(u):
        for j, d in enumerate(PAIRS[u]):
            p = source(d)
            arrived(kvg.at[p, 1 - c], c_s.at[d], c_r.at[d])
            both = kvg[p].reshape(CHUNKS, 16, DH).astype(F32).reshape(CHUNKS, 2, TOK, DH)
            k = both[:, 0].reshape(KEYS, DH).astype(BF16)
            ks[j * KEYS:(j + 1) * KEYS, :] = k
            kt[u, :, j * KEYS:(j + 1) * KEYS] = k.T
            vs[j * KEYS:(j + 1) * KEYS, :] = both[:, 1].reshape(KEYS, DH).astype(BF16)

        def tile(t, carry):
            limit = (lane // GROUP) % TOK + (y % 2) * 32
            for j in range(2):
                zs = got_from(2 * t + j, z)
                first = order_ref[(zs // 4) * 16 + x * 4 + c * 2 + y // 2] * 64 + (zs % 4) * 8
                limit = limit + jnp.where(lane // DH == j, first, 0)
            s = dot(ks[...], qt[t])
            at = jnp.concatenate((pos[PAIRS[u][0]], pos[PAIRS[u][1]]), axis=0)
            s = jnp.where(jnp.concatenate((at, at), axis=1) <= limit, s, -1e30)
            old = top[t]
            new = jnp.maximum(old, jnp.max(s, axis=0, keepdims=True))
            e = jnp.exp2((s - new) * RATE)
            prob[u, t] = e
            dp = dot(vs[...], gt[t])
            dprob[u, t] = dp
            fade = jnp.exp2((old - new) * RATE)
            total[t] = total[t] * fade + jnp.sum(e, axis=0, keepdims=True)
            mixed[t] = mixed[t] * fade + jnp.sum(e * dp, axis=0, keepdims=True)
            tops[u, t] = new
            top[t] = new
            return carry

        lax.fori_loop(0, TILES, tile, 0, unroll=4)

    for u in range(UNITS):
        for d in PAIRS[u]:
            swap(d)
        if u == 1:
            take_queries()
        if u >= 1:
            score(u - 1)
    score(UNITS - 1)
    total[...] = 1.0 / total[...]
    mixed[...] = mixed[...] * total[...]

    def grads(u):
        dk[...] = jnp.zeros_like(dk)
        dv[...] = jnp.zeros_like(dv)

        def tile(t, carry):
            share_of = jnp.exp2((tops[u, t] - top[t]) * RATE) * total[t]
            p = prob[u, t] * share_of
            ds = (p * (dprob[u, t] - mixed[t])).astype(BF16)
            dv[...] += dot(p.astype(BF16), ga[pl.ds(2 * t, 2)].reshape(TR, DH))
            dk[...] += dot(ds, qa[pl.ds(2 * t, 2)].reshape(TR, DH))
            dqt[t] += dot(kt[u], ds)
            return carry

        lax.fori_loop(0, TILES, tile, 0, unroll=4)
        for j, d in enumerate(PAIRS[u]):
            rows = slice(j * KEYS, (j + 1) * KEYS)
            both = jnp.stack(((dk[rows, :] * SCALE).reshape(CHUNKS, TOK, DH), dv[rows, :].reshape(CHUNKS, TOK, DH)), axis=1)
            dkv[d] = both.reshape(2, NZ, 16, DH).astype(BF16)
            start(dkv.at[d, 1 - c], cx.at[d], d_s.at[d], d_r.at[d], other)

    def along(u):
        for d in PAIRS[u]:
            arrived(cx.at[d], d_s.at[d], d_r.at[d])
            if d:
                back = opposite(d)
                pst[d] = (dkv[d, c].astype(F32) + cx[d].astype(F32)).astype(BF16)
                start(pst.at[d], pr.at[back], e_s.at[back], e_r.at[back], away(back))

    late = tuple(reversed(range(UNITS)))
    for k, u in enumerate(late):
        grads(u)
        if k:
            along(late[k - 1])
    along(late[-1])
    for t in range(TILES):
        dqs[2 * t:2 * t + 2] = (dqt[t] * SCALE).T.astype(BF16).reshape(2, TOK, GROUP, DH)
    rows = pl.ds(head * GROUP, GROUP)
    dq_own = local(dqs.at[0], dqh_ref.at[:, rows, :], 2)
    for o in range(1, HEADS):
        start(dqs.at[o], dqh_ref.at[:, rows, :], o_s.at[o], o_r.at[o], device(x, y, got_from(o, z), c))
    part = dkv[0, c].astype(F32) + cx[0].astype(F32)
    for u in late:
        for d in PAIRS[u]:
            if d:
                arrived(pr.at[d], e_s.at[d], e_r.at[d])
                part = part + pr[d].astype(F32)
    fst[...] = part.astype(BF16)
    for d in reversed(OUTWARD):
        start(fst.at[(HERE + d) % NZ], fin.at[z], f_s.at[d], f_r.at[d], device(x, y, (z + d) % NZ, c))
    kv_home = local(fst.at[HERE], fin.at[z], 4)
    kv_home.wait()
    for d in range(1, NZ):
        arrived(fin.at[(z + NZ - d) % NZ], f_s.at[d], f_r.at[d])
    home = fin[:HEADS].astype(F32) + fin[HEADS:].astype(F32)
    dkh_ref[...] = jnp.swapaxes(home[:, :TOK], 0, 1).astype(BF16)
    dvh_ref[...] = jnp.swapaxes(home[:, TOK:], 0, 1).astype(BF16)
    dq_own.wait()
    for o in range(1, HEADS):
        arrived(dqh_ref.at[:, pl.ds(given_to(o, z) % HEADS * GROUP, GROUP), :], o_s.at[o], o_r.at[o])
    for one in sends:
        one.wait_send()


def backward(order, query, key, value, out_grad):
    sem = pltpu.SemaphoreType.DMA
    hbm = pl.BlockSpec(memory_space=pl.ANY)
    vmem = pl.BlockSpec(memory_space=pltpu.VMEM)
    block = (NZ, 16, DH)
    rows = (HEADS, TOK, GROUP, DH)
    home = (TOK, HEADS, DH)
    stat = pltpu.VMEM((TILES, 1, TR), F32)
    eight, many, both = sem((HEADS,)), sem((NZ,)), sem((2, PLANE))
    return pl.pallas_call(
        kernel,
        out_shape=(
            jax.ShapeDtypeStruct((TOK, HEADS * GROUP, DH), BF16),
            jax.ShapeDtypeStruct(home, BF16),
            jax.ShapeDtypeStruct(home, BF16),
        ),
        in_specs=[pl.BlockSpec(memory_space=pltpu.SMEM), hbm, hbm, hbm, hbm],
        out_specs=[vmem, vmem, vmem],
        scratch_shapes=[
            pltpu.VMEM(home, BF16), pltpu.VMEM(home, BF16), pltpu.VMEM((HEADS, 16, DH), BF16),
            pltpu.VMEM(rows, BF16), pltpu.VMEM(rows, BF16),
            pltpu.VMEM((TILES, DH, TR), BF16), pltpu.VMEM((TILES, DH, TR), BF16),
            pltpu.VMEM((PLANE, 2) + block, BF16),
            pltpu.VMEM((2 * KEYS, DH), BF16), pltpu.VMEM((2 * KEYS, DH), BF16), pltpu.VMEM((UNITS, DH, 2 * KEYS), BF16),
            pltpu.VMEM((PLANE, KEYS, DH), jnp.int32),
            pltpu.VMEM((UNITS, TILES, 2 * KEYS, TR), F32), pltpu.VMEM((UNITS, TILES, 2 * KEYS, TR), F32),
            pltpu.VMEM((UNITS, TILES, 1, TR), F32), stat, stat, stat,
            pltpu.VMEM((2 * KEYS, DH), F32), pltpu.VMEM((2 * KEYS, DH), F32),
            pltpu.VMEM((TILES, DH, TR), F32), pltpu.VMEM(rows, BF16),
            pltpu.VMEM((PLANE, 2) + block, BF16), pltpu.VMEM((PLANE,) + block, BF16),
            pltpu.VMEM((PLANE,) + block, BF16), pltpu.VMEM((PLANE,) + block, BF16),
            pltpu.VMEM(block, BF16), pltpu.VMEM(block, BF16),
            many, many, both, both, many, many, eight, eight, eight, eight,
            many, many, many, many, many, many, eight, eight, sem((5,)),
        ],
        compiler_params=pltpu.CompilerParams(collective_id=0, has_side_effects=True, vmem_limit_bytes=58 << 20),
        name="attention_backward",
    )(order, query, key, value, out_grad)


def on_device(query, key, value, out_grad, block_order):
    return backward(block_order, query, key, value, out_grad)


def solution(mesh):
    rows = P(("blk", "head"), None, None)
    return jax.shard_map(
        on_device, mesh=mesh, in_specs=(rows,) * 4 + (P(),), out_specs=(rows,) * 3, check_vma=False
    )
```

```python
import math

import jax
import jax.numpy as jnp
from jax import lax
from jax.experimental import pallas as pl
from jax.experimental.pallas import tpu as pltpu
from jax.sharding import PartitionSpec as P

MESH = pl.DeviceIdType.MESH
F32 = jnp.float32
BF16 = jnp.bfloat16
NX, NY, NZ = 4, 4, 16
PLANE = NX * NY
HEADS = 8
TOK = 8
GROUP = 16
DH = 128
TILES = 4
TR = HEADS * TOK * GROUP // TILES
CHUNKS = 2 * NZ
KEYS = CHUNKS * TOK
SCALE = DH ** -0.5
RATE = SCALE * math.log2(math.e)
PART = KEYS // 2
QUADS = ((0, 1, 3, 4), (12, 5, 15, 7), (13, 2, 8, 6), (14, 9, 11, 10))
UNITS = 2 * len(QUADS)
NEAR = tuple(d for quad in QUADS for d in quad if d)
HERE = 4
HALF = NZ // 2
SLOTS = (slice(0, HALF), slice(HALF, NZ))
OUTWARD = (1, 15, 2, 14, 3, 13, 4, 12, 5, 11, 6, 10, 7, 9, 8)


def unit(u):
    return u // len(QUADS), QUADS[u % len(QUADS)]


def opposite(d):
    return (NX - d // NY) % NX * NY + (NY - d % NY) % NY


def place():
    blk = lax.axis_index("blk")
    head = lax.axis_index("head")
    z = (blk // 8) * 4 + head % 4
    return (blk // 2) % 4, head // 4, z, blk % 2


def device(x, y, z, c):
    return (((z // 4) * 4 + x) * 2 + c, y * 4 + z % 4)


def turn(o, z):
    return 8 * ((o + 3) // 8) + 8 * (z % 2) * (o // 4 - (o + 3) // 8)


def given_to(o, z):
    return (z + o + turn(o, z)) % NZ


def got_from(o, z):
    return (z + NZ - o + turn(o, z)) % NZ


def dot(a, b):
    return lax.dot_general(a, b, (((1,), (0,)), ((), ())), preferred_element_type=F32)


def kernel(
    order_ref, q_ref, k_ref, v_ref, g_ref, dqh_ref, dkh_ref, dvh_ref,
    kin, vin, kv, qa, ga, qt, gt, kvg, ks, vs, kt, pos, prob, dprob, tops, top, total, mixed, dk, dv, dqt, dqs,
    dkv, cx, pst, pr, fst, fin,
    k_s, k_r, p_s, p_r, c_s, c_r, q_s, q_r, g_s, g_r, d_s, d_r, e_s, e_r, f_s, f_r, o_s, o_r, own,
):
    x, y, z, c = place()
    i = x * NY + y
    head = z % HEADS
    other = device(x, y, z, 1 - c)
    sends = []

    def copy(src, dst, ss, rs, to):
        return pltpu.make_async_remote_copy(
            src_ref=src, dst_ref=dst, send_sem=ss, recv_sem=rs, device_id=to, device_id_type=MESH
        )

    def start(src, dst, ss, rs, to):
        one = copy(src, dst, ss, rs, to)
        one.start()
        sends.append(one)

    def arrived(dst, ss, rs):
        copy(dst, dst, ss, rs, other).wait_recv()

    def local(src, dst, at):
        one = pltpu.make_async_copy(src, dst, own.at[at])
        one.start()
        return one

    def away(d):
        return device((x + d // NY) % NX, (y + d % NY) % NY, z, c)

    def source(d):
        return (x + NX - d // NY) % NX * NY + (y + NY - d % NY) % NY

    barrier = pltpu.get_barrier_semaphore()
    to = [device(x, y, (z + d) % NZ, c) for d in range(1, NZ)]
    to += [away(d) for d in range(1, PLANE)]
    to += [other]
    for one in to:
        pl.semaphore_signal(barrier, inc=1, device_id=one, device_id_type=MESH)

    k_in = local(k_ref, kin, 0)
    v_in = local(v_ref, vin, 1)
    q_own = local(q_ref.at[:, pl.ds(head * GROUP, GROUP), :], qa.at[0], 2)
    g_own = local(g_ref.at[:, pl.ds(head * GROUP, GROUP), :], ga.at[0], 3)
    k_in.wait()
    v_in.wait()
    kv[...] = jnp.concatenate(
        (jnp.swapaxes(kin[...].astype(F32), 0, 1), jnp.swapaxes(vin[...].astype(F32), 0, 1)), axis=1
    ).astype(BF16)
    kv_own = local(kv.at[head], kvg.at[i, c, HERE], 4)

    pl.semaphore_wait(barrier, len(to))

    for d in OUTWARD:
        zd = (z + d) % NZ
        start(kv.at[zd % HEADS], kvg.at[i, c, (HERE - d) % NZ], k_s.at[d], k_r.at[d], device(x, y, zd, c))
    for o in range(1, HEADS):
        zd = given_to(o, z)
        rows = pl.ds(zd % HEADS * GROUP, GROUP)
        start(q_ref.at[:, rows, :], qa.at[o], q_s.at[o], q_r.at[o], device(x, y, zd, c))
        start(g_ref.at[:, rows, :], ga.at[o], g_s.at[o], g_r.at[o], device(x, y, zd, c))

    step = lax.broadcasted_iota(jnp.int32, (TOK, DH), 0)

    def place_keys(d, carry):
        xs = (x + NX - d // NY) % NX
        ys = (y + NY - d % NY) % NY
        for cc in range(2):
            for zz in range(NZ):
                zs = (z + NZ + zz - HERE) % NZ
                first = order_ref[(zs // 4) * 16 + xs * 4 + cc * 2 + ys // 2] * 64 + (ys % 2) * 32 + (zs % 4) * 8
                at = (cc * HALF + zz % HALF) * TOK
                pos[zz // HALF, d, at:at + TOK, :] = first + step
        return carry

    lax.fori_loop(0, PLANE, place_keys, 0)
    top[...] = jnp.full_like(top, -1e30)
    total[...] = jnp.zeros_like(total)
    mixed[...] = jnp.zeros_like(mixed)
    dqt[...] = jnp.zeros_like(dqt)

    kv_own.wait()
    for part, slots in enumerate(SLOTS):
        for d in OUTWARD:
            if (HERE - d) % NZ // HALF == part:
                arrived(kvg.at[i, c, (HERE - d) % NZ], k_s.at[d], k_r.at[d])
        for d in NEAR:
            block = kvg.at[i, c, slots]
            start(block, block, p_s.at[part, d], p_r.at[part, d], away(d))
        block = kvg.at[i, c, slots]
        start(block, block, c_s.at[part, 0], c_r.at[part, 0], other)

    lane = lax.broadcasted_iota(jnp.int32, (1, TR), 1)

    def take_queries():
        q_own.wait()
        g_own.wait()
        for o in range(1, HEADS):
            arrived(qa.at[o], q_s.at[o], q_r.at[o])
            arrived(ga.at[o], g_s.at[o], g_r.at[o])
        for t in range(TILES):
            qt[t] = qa[2 * t:2 * t + 2].reshape(TR, DH).T
            gt[t] = ga[2 * t:2 * t + 2].reshape(TR, DH).T

    def swap(part, d):
        if d:
            block = kvg.at[source(d), c, SLOTS[part]]
            arrived(block, p_s.at[part, d], p_r.at[part, d])
            start(block, block, c_s.at[part, d], c_r.at[part, d], other)

    def score(u):
        part, places = unit(u)
        for j, d in enumerate(places):
            p = source(d)
            arrived(kvg.at[p, 1 - c, SLOTS[part]], c_s.at[part, d], c_r.at[part, d])
            both = kvg[p, :, SLOTS[part]].reshape(2 * HALF, 16, DH).astype(F32).reshape(2 * HALF, 2, TOK, DH)
            rows = slice(j * PART, (j + 1) * PART)
            k = both[:, 0].reshape(PART, DH).astype(BF16)
            ks[rows, :] = k
            kt[u, :, rows] = k.T
            vs[rows, :] = both[:, 1].reshape(PART, DH).astype(BF16)

        def tile(t, carry):
            limit = (lane // GROUP) % TOK + (y % 2) * 32
            for j in range(2):
                zs = got_from(2 * t + j, z)
                first = order_ref[(zs // 4) * 16 + x * 4 + c * 2 + y // 2] * 64 + (zs % 4) * 8
                limit = limit + jnp.where(lane // DH == j, first, 0)
            s = dot(ks[...], qt[t])
            at = jnp.concatenate([pos[part, d] for d in places], axis=0)
            s = jnp.where(jnp.concatenate((at, at), axis=1) <= limit, s, -1e30)
            old = top[t]
            new = jnp.maximum(old, jnp.max(s, axis=0, keepdims=True))
            e = jnp.exp2((s - new) * RATE)
            prob[u, t] = e
            dp = dot(vs[...], gt[t])
            dprob[u, t] = dp
            fade = jnp.exp2((old - new) * RATE)
            total[t] = total[t] * fade + jnp.sum(e, axis=0, keepdims=True)
            mixed[t] = mixed[t] * fade + jnp.sum(e * dp, axis=0, keepdims=True)
            tops[u, t] = new
            top[t] = new
            return carry

        lax.fori_loop(0, TILES, tile, 0, unroll=4)

    for u in range(UNITS):
        for d in unit(u)[1]:
            swap(unit(u)[0], d)
        if u == 1:
            take_queries()
        if u >= 1:
            score(u - 1)
    score(UNITS - 1)
    total[...] = 1.0 / total[...]
    mixed[...] = mixed[...] * total[...]

    def grads(u):
        dk[...] = jnp.zeros_like(dk)
        dv[...] = jnp.zeros_like(dv)

        def tile(t, carry):
            share_of = jnp.exp2((tops[u, t] - top[t]) * RATE) * total[t]
            p = prob[u, t] * share_of
            ds = (p * (dprob[u, t] - mixed[t])).astype(BF16)
            dv[...] += dot(p.astype(BF16), ga[pl.ds(2 * t, 2)].reshape(TR, DH))
            dk[...] += dot(ds, qa[pl.ds(2 * t, 2)].reshape(TR, DH))
            dqt[t] += dot(kt[u], ds)
            return carry

        lax.fori_loop(0, TILES, tile, 0, unroll=4)
        part, places = unit(u)
        for j, d in enumerate(places):
            rows = slice(j * PART, (j + 1) * PART)
            both = jnp.stack(
                ((dk[rows, :] * SCALE).reshape(2 * HALF, TOK, DH), dv[rows, :].reshape(2 * HALF, TOK, DH)), axis=1
            )
            dkv[d, :, SLOTS[part]] = both.reshape(2, HALF, 16, DH).astype(BF16)
            start(dkv.at[d, 1 - c, SLOTS[part]], cx.at[d, SLOTS[part]], d_s.at[part, d], d_r.at[part, d], other)

    def along(u):
        part, places = unit(u)
        slots = SLOTS[part]
        for d in places:
            arrived(cx.at[d, slots], d_s.at[part, d], d_r.at[part, d])
            if d:
                back = opposite(d)
                pst[d, slots] = (dkv[d, c, slots].astype(F32) + cx[d, slots].astype(F32)).astype(BF16)
                start(pst.at[d, slots], pr.at[back, slots], e_s.at[part, back], e_r.at[part, back], away(back))

    def finish(part):
        slots = SLOTS[part]
        here = dkv[0, c, slots].astype(F32) + cx[0, slots].astype(F32)
        for d in reversed(NEAR):
            arrived(pr.at[d, slots], e_s.at[part, d], e_r.at[part, d])
            here = here + pr[d, slots].astype(F32)
        fst[slots] = here.astype(BF16)
        for d in reversed(OUTWARD):
            at = (HERE + d) % NZ
            if at // HALF == part:
                start(fst.at[at], fin.at[z], f_s.at[d], f_r.at[d], device(x, y, (z + d) % NZ, c))

    late = tuple(reversed(range(UNITS)))
    for k, u in enumerate(late):
        grads(u)
        if k:
            along(late[k - 1])
    along(late[-1])
    finish(1)
    for t in range(TILES):
        dqs[2 * t:2 * t + 2] = (dqt[t] * SCALE).T.astype(BF16).reshape(2, TOK, GROUP, DH)
    rows = pl.ds(head * GROUP, GROUP)
    dq_own = local(dqs.at[0], dqh_ref.at[:, rows, :], 2)
    for o in range(1, HEADS):
        start(dqs.at[o], dqh_ref.at[:, rows, :], o_s.at[o], o_r.at[o], device(x, y, got_from(o, z), c))
    finish(0)
    kv_home = local(fst.at[HERE], fin.at[z], 4)
    kv_home.wait()
    for d in range(1, NZ):
        arrived(fin.at[(z + NZ - d) % NZ], f_s.at[d], f_r.at[d])
    home = fin[:HEADS].astype(F32) + fin[HEADS:].astype(F32)
    dkh_ref[...] = jnp.swapaxes(home[:, :TOK], 0, 1).astype(BF16)
    dvh_ref[...] = jnp.swapaxes(home[:, TOK:], 0, 1).astype(BF16)
    dq_own.wait()
    for o in range(1, HEADS):
        arrived(dqh_ref.at[:, pl.ds(given_to(o, z) % HEADS * GROUP, GROUP), :], o_s.at[o], o_r.at[o])
    for one in sends:
        one.wait_send()


def backward(order, query, key, value, out_grad):
    sem = pltpu.SemaphoreType.DMA
    hbm = pl.BlockSpec(memory_space=pl.ANY)
    vmem = pl.BlockSpec(memory_space=pltpu.VMEM)
    block = (NZ, 16, DH)
    rows = (HEADS, TOK, GROUP, DH)
    home = (TOK, HEADS, DH)
    stat = pltpu.VMEM((TILES, 1, TR), F32)
    eight, many, both = sem((HEADS,)), sem((NZ,)), sem((2, PLANE))
    return pl.pallas_call(
        kernel,
        out_shape=(
            jax.ShapeDtypeStruct((TOK, HEADS * GROUP, DH), BF16),
            jax.ShapeDtypeStruct(home, BF16),
            jax.ShapeDtypeStruct(home, BF16),
        ),
        in_specs=[pl.BlockSpec(memory_space=pltpu.SMEM), hbm, hbm, hbm, hbm],
        out_specs=[vmem, vmem, vmem],
        scratch_shapes=[
            pltpu.VMEM(home, BF16), pltpu.VMEM(home, BF16), pltpu.VMEM((HEADS, 16, DH), BF16),
            pltpu.VMEM(rows, BF16), pltpu.VMEM(rows, BF16),
            pltpu.VMEM((TILES, DH, TR), BF16), pltpu.VMEM((TILES, DH, TR), BF16),
            pltpu.VMEM((PLANE, 2) + block, BF16),
            pltpu.VMEM((2 * KEYS, DH), BF16), pltpu.VMEM((2 * KEYS, DH), BF16), pltpu.VMEM((UNITS, DH, 2 * KEYS), BF16),
            pltpu.VMEM((2, PLANE, PART, DH), jnp.int32),
            pltpu.VMEM((UNITS, TILES, 2 * KEYS, TR), F32), pltpu.VMEM((UNITS, TILES, 2 * KEYS, TR), F32),
            pltpu.VMEM((UNITS, TILES, 1, TR), F32), stat, stat, stat,
            pltpu.VMEM((2 * KEYS, DH), F32), pltpu.VMEM((2 * KEYS, DH), F32),
            pltpu.VMEM((TILES, DH, TR), F32), pltpu.VMEM(rows, BF16),
            pltpu.VMEM((PLANE, 2) + block, BF16), pltpu.VMEM((PLANE,) + block, BF16),
            pltpu.VMEM((PLANE,) + block, BF16), pltpu.VMEM((PLANE,) + block, BF16),
            pltpu.VMEM(block, BF16), pltpu.VMEM(block, BF16),
            many, many, both, both, both, both, eight, eight, eight, eight,
            both, both, both, both, many, many, eight, eight, sem((5,)),
        ],
        compiler_params=pltpu.CompilerParams(collective_id=0, has_side_effects=True, vmem_limit_bytes=58 << 20),
        name="attention_backward",
    )(order, query, key, value, out_grad)


def on_device(query, key, value, out_grad, block_order):
    return backward(block_order, query, key, value, out_grad)


def solution(mesh):
    rows = P(("blk", "head"), None, None)
    return jax.shard_map(
        on_device, mesh=mesh, in_specs=(rows,) * 4 + (P(),), out_specs=(rows,) * 3, check_vma=False
    )
```
